32 devices in a mesh: groups: 2 (over y), pair: 4 (over z), aux: 2 (over x), occ: 2 (over core).
Axes of the slice: x: 2, y: 2, z: 4, core: 2. Of those that a mesh axis runs over, the one named last changes fastest.
Arguments:
- three_index: bfloat16 [48, 20480, 256], P(('groups', 'pair', 'occ'), 'aux'), parts along dimension 0, may hold values from -1.25 to 1.25
- pair_orbs: int32 [128, 2], P('groups'), parts along dimension 0, may hold values from 0 to 23, as said below
- live_pairs: int32 [16], P('groups'), parts along dimension 0, may hold values from 1 to 8, as said below
- domains: int32 [48, 256], P('groups'), parts along dimension 0, may hold values from 0 to 1791, as said below
- coupled: int32 [128, 4], P(('groups', 'pair', 'occ')), parts along dimension 0, may hold values from 0 to 63, as said below
- fock_coupling_weight: float32 [128, 4], P(('groups', 'pair', 'occ')), parts along dimension 0, may hold values from -4 to 4
- occ_energy: float32 [48], P('groups'), parts along dimension 0, may hold values from -1.2 to -0.3
- virt_energy: float32 [3584], P('groups'), parts along dimension 0, may hold values from 0.4 to 4
Outputs:
- amplitudes: bfloat16 [128, 256, 256], P(('groups', 'pair', 'occ')), parts along dimension 0
The draws below stay inside these ranges and needn't reach their ends.
There are 2 independent parts, one for each index of `groups`. The reference program is written for one: setup_inputs(seed, part) draws one part's arguments, and reference() takes and returns one part's arrays. A program takes and returns all parts, laid end to end along the dimension named above; each array names one. Nothing has to cross between parts.
Inputs may be any that keep to these rules, and one draw needn't show every extreme that they name: pair_orbs[s, 0] is an orbital of owner s // 8 (orbitals o * 3 to o * 3 + 2 belong to owner o); pair_orbs[s, 1] differs from it and belongs to the same owner or to one of the two owners beside it; pairs may repeat. The live slots of an owner are its first live_pairs[o] slots; some owner has all 8 slots live. `domains`: each row holds 256 distinct virtual indices. `coupled`: each entry is a live slot of the same owner or of one of the two owners beside it.
All inputs are finite; a program needn't handle non-finite values.
Results may differ from the reference program's by a relative error of at most 0.0045.
Values may be sent and summed in bfloat16 or wider, within the bound.
No kernel may reach another device: no remote copies, remote signals or barrier semaphores. Data moves between devices by JAX's collectives and lax.ppermute only.
A program may use at most 192 MiB of HBM per device.

```python
import math
import jax
import jax.numpy as jnp
from jax import lax

DV = 256
NAUX = 20480
OWNER_ORBITALS = 3
OWNER_PAIRS = 8
NEIGHBOUR_COUNT = 4
ITERS = 2
NOWN = 8
NOCC = 24
WINDOW_SLOTS = 64
NVIRT = 1792


def live_counts(key):
    count_key, top_key = jax.random.split(jax.random.fold_in(key, 101))
    pair_counts = jax.random.randint(count_key, (NOWN,), 1, OWNER_PAIRS + 1)
    busiest = jax.random.randint(top_key, (), 0, NOWN)
    return pair_counts.at[busiest].set(OWNER_PAIRS).astype(jnp.int32)


def draw_live_pairs(key, part):
    return live_counts(key)


def draw_pair_orbs(key, part):
    key = jax.random.fold_in(key, 7)
    row_random_key, column_key = jax.random.split(key)
    slot_indices = jnp.arange(WINDOW_SLOTS, dtype=jnp.int32)
    owner_list = slot_indices // OWNER_PAIRS
    row_orbitals = owner_list * OWNER_ORBITALS + jax.random.randint(row_random_key, (WINDOW_SLOTS,), 0, OWNER_ORBITALS)
    pair_band = jax.random.randint(column_key, (WINDOW_SLOTS,), 0, 3 * OWNER_ORBITALS - 1)
    lowest = jnp.clip((owner_list - 1) * OWNER_ORBITALS, 0, NOCC)
    highest = jnp.clip((owner_list + 2) * OWNER_ORBITALS, 0, NOCC)
    spread = highest - lowest - 1
    col_orbs = lowest + pair_band % spread
    col_orbs = jnp.where(col_orbs >= row_orbitals, col_orbs + 1, col_orbs)
    return jnp.stack([row_orbitals, col_orbs], axis=1).astype(jnp.int32)


def draw_domains(key, part):
    key = jax.random.fold_in(key, 11)
    shift_key, order_key = jax.random.split(key)
    shifts = jax.random.randint(shift_key, (NOCC,), 0, DV // 4 + 1)
    shifts = shifts.at[0].set(0).at[NOCC - 1].set(DV // 4)
    orders = jax.vmap(lambda k: jax.random.permutation(k, DV))(jax.random.split(order_key, NOCC))
    bases = jnp.arange(NOCC, dtype=jnp.int32) * (DV // 4) + shifts
    return (bases[:, None] + orders).astype(jnp.int32)


def draw_coupled(key, part):
    pair_counts = live_counts(key)
    key = jax.random.fold_in(key, 13)
    side_random_key, selection_key = jax.random.split(key)
    owner_list = jnp.arange(WINDOW_SLOTS, dtype=jnp.int32) // OWNER_PAIRS
    pair_sides = jax.random.randint(side_random_key, (WINDOW_SLOTS, NEIGHBOUR_COUNT), -1, 2)
    source_slots = jnp.clip(owner_list[:, None] + pair_sides, 0, NOWN - 1)
    picked_pairs = jax.random.randint(selection_key, (WINDOW_SLOTS, NEIGHBOUR_COUNT), 0, 1 << 20) % pair_counts[source_slots]
    return (source_slots * OWNER_PAIRS + picked_pairs).astype(jnp.int32)


def steps_of(rng, shape, shards, low, largest):
    level, own = 1.0, jax.random.fold_in(rng, 6)
    for position, blocks in shards:
        draws = jnp.exp(jax.random.uniform(jax.random.fold_in(own, position), (blocks,), jnp.float32, low / len(shards), largest / len(shards)))
        level = level * jnp.repeat(draws, shape[position] // blocks).reshape([-1 if axis == position else 1 for axis in range(len(shape))])
    return level


def noise(own_key, extent, scale, reach, cuts=(), held_as=jnp.bfloat16):
    values = jax.random.normal(own_key, extent, jnp.float32) * scale
    if len(cuts) > 0:
        values = steps_of(own_key, extent, cuts, -0.22, 0.18) * values
    return jnp.clip(values, min=-reach, max=reach).astype(held_as)


def setup_inputs(seed: int = 0, part: int = 0) -> dict:
    streams_of = jax.random.split(jax.random.key(seed), 9)
    part_splits = jax.random.split(jax.random.fold_in(streams_of[8], part), 9)
    three_index = noise(part_splits[0], (NOCC, NAUX, DV), (NAUX ** -0.25), 1.25, ((0, 8), (1, 2)))
    pair_orbs = draw_pair_orbs(jax.random.fold_in(jax.random.fold_in(streams_of[8], part), 71), part)
    live_pairs = draw_live_pairs(jax.random.fold_in(jax.random.fold_in(streams_of[8], part), 71), part)
    domains = draw_domains(jax.random.fold_in(jax.random.fold_in(streams_of[8], part), 71), part)
    coupled = draw_coupled(jax.random.fold_in(jax.random.fold_in(streams_of[8], part), 71), part)
    fock_coupling_weight = jnp.clip(jax.random.uniform(part_splits[5], (WINDOW_SLOTS, NEIGHBOUR_COUNT), jnp.float32, -4.0, 4.0) * steps_of(part_splits[5], (WINDOW_SLOTS, NEIGHBOUR_COUNT), ((0, 8),), -0.4, 0.0), -4.0, 4.0)
    occ_energy = jnp.clip(jax.random.uniform(part_splits[6], (NOCC,), jnp.float32, -1.2, -0.3), -1.2, -0.3)
    virt_energy = jnp.clip(jnp.exp(jax.random.uniform(part_splits[7], (NVIRT,), jnp.float32, math.log(0.4), math.log(4.0))), 0.4, 4.0)
    return dict(three_index=three_index, pair_orbs=pair_orbs, live_pairs=live_pairs, domains=domains, coupled=coupled, fock_coupling_weight=fock_coupling_weight, occ_energy=occ_energy, virt_energy=virt_energy)


def match_table(left_dom, right_dom):
    return (left_dom[:, None] == right_dom[None, :]).astype(jnp.bfloat16)


def reference(three_index, pair_orbs, live_pairs, domains, coupled, fock_coupling_weight, occ_energy, virt_energy):
    slot_indices = jnp.arange(WINDOW_SLOTS, dtype=jnp.int32)
    owner_list = slot_indices // OWNER_PAIRS
    live_mask = (slot_indices % OWNER_PAIRS < live_pairs[owner_list]).astype(jnp.float32)

    def integral(slot_id):
        left_block = three_index[pair_orbs[slot_id, 0]]
        right_block = three_index[pair_orbs[slot_id, 1]]
        return jnp.dot(left_block.T, right_block, preferred_element_type=jnp.float32)

    integrals = lax.map(integral, slot_indices) * live_mask[:, None, None]

    def denominator(slot_id):
        row_orb = pair_orbs[slot_id, 0]
        col_orb = pair_orbs[slot_id, 1]
        row_energy = virt_energy[domains[row_orb]]
        col_energy = virt_energy[domains[col_orb]]
        return row_energy[:, None] + col_energy[None, :] - occ_energy[row_orb] - occ_energy[col_orb]

    denominators = lax.map(denominator, slot_indices)
    amplitudes = -integrals / denominators
    for sweep in range(ITERS):
        rounded = amplitudes.astype(jnp.bfloat16)

        def couple(slot_id):
            row_dom = domains[pair_orbs[slot_id, 0]]
            col_dom = domains[pair_orbs[slot_id, 1]]
            summed = jnp.zeros((DV, DV), jnp.float32)
            for which in range(NEIGHBOUR_COUNT):
                source_slot = coupled[slot_id, which]
                row_match = match_table(row_dom, domains[pair_orbs[source_slot, 0]])
                col_match = match_table(domains[pair_orbs[source_slot, 1]], col_dom)
                selected = jnp.dot(row_match, rounded[source_slot], preferred_element_type=jnp.float32).astype(jnp.bfloat16)
                summed = summed + fock_coupling_weight[slot_id, which] * jnp.dot(selected, col_match, preferred_element_type=jnp.float32)
            return summed

        coupling = lax.map(couple, slot_indices)
        amplitudes = live_mask[:, None, None] * (coupling - integrals) / denominators
    return amplitudes.astype(jnp.bfloat16)
```

```python
import functools

import jax
import jax.numpy as jnp
from jax import lax
from jax.experimental import pallas as pl
from jax.experimental.pallas import tpu as pltpu
from jax.sharding import PartitionSpec as P

ITERS = 2
LINE = ("pair", "occ")
VMEM = 56 * 1024 * 1024
F32 = jnp.float32
BF16 = jnp.bfloat16
ROWS = (((0,), (0,)), ((), ()))


def chip_mate(value):
    return lax.ppermute(value, "occ", [(0, 1), (1, 0)])


def line_mate(value):
    pairs = []
    for chip in range(lax.axis_size("pair") - 1):
        left, right = 2 * chip + 1, 2 * chip + 2
        pairs += [(left, right), (right, left)]
    return lax.ppermute(value, LINE, pairs)


def aux_sum(value):
    count = lax.axis_size("aux")
    step = 1
    while step < count:
        other = lax.ppermute(value, "aux", [(i, i ^ step) for i in range(count)])
        value = (value.astype(F32) + other.astype(F32)).astype(BF16)
        step *= 2
    return value


def tile_rows(rows):
    for tile in (1280, 1024, 640, 512, 256, 128):
        if rows % tile == 0:
            return tile
    return rows


def own_kernel(block_ref, out_ref, total_ref):
    step = pl.program_id(0)

    @pl.when(step == 0)
    def _():
        total_ref[...] = jnp.zeros_like(total_ref)

    count = block_ref.shape[0]
    at = 0
    for left in range(count):
        for right in range(left + 1, count):
            total_ref[at] += lax.dot_general(block_ref[left], block_ref[right], ROWS, preferred_element_type=F32)
            at += 1

    @pl.when(step == pl.num_programs(0) - 1)
    def _():
        out_ref[...] = total_ref[...].astype(out_ref.dtype)


def own_products(blocks):
    count, rows, width = blocks.shape
    tile = tile_rows(rows)
    combos = count * (count - 1) // 2
    return pl.pallas_call(
        own_kernel,
        grid=(rows // tile,),
        in_specs=[pl.BlockSpec((count, tile, width), lambda t: (0, t, 0))],
        out_specs=pl.BlockSpec((combos, width, width), lambda t: (0, 0, 0)),
        out_shape=jax.ShapeDtypeStruct((combos, width, width), BF16),
        scratch_shapes=[pltpu.VMEM((combos, width, width), F32)],
        compiler_params=pltpu.CompilerParams(vmem_limit_bytes=VMEM),
        cost_estimate=pl.CostEstimate(
            flops=2 * combos * rows * width * width, bytes_accessed=2 * count * rows * width, transcendentals=0
        ),
        name="own_products",
    )(blocks)


def mate_kernel(half_ref, block_ref, mate_ref, out_ref, total_ref):
    step = pl.program_id(0)

    @pl.when(step == 0)
    def _():
        total_ref[...] = jnp.zeros_like(total_ref)

    mate = mate_ref[...]
    for orb in range(block_ref.shape[0]):
        total_ref[orb] += lax.dot_general(mate, block_ref[orb], ROWS, preferred_element_type=F32)

    @pl.when(step == pl.num_programs(0) - 1)
    def _():
        out_ref[...] = total_ref[...].astype(out_ref.dtype)


def mate_products(half, blocks, mate):
    count, _, width = blocks.shape
    rows, cols = mate.shape
    tile = tile_rows(rows)
    steps = rows // tile
    return pl.pallas_call(
        mate_kernel,
        grid_spec=pltpu.PrefetchScalarGridSpec(
            num_scalar_prefetch=1,
            grid=(steps,),
            in_specs=[
                pl.BlockSpec((count, tile, width), lambda t, half: (0, half[0] * steps + t, 0)),
                pl.BlockSpec((tile, cols), lambda t, half: (t, 0)),
            ],
            out_specs=pl.BlockSpec((count, cols, width), lambda t, half: (0, 0, 0)),
            scratch_shapes=[pltpu.VMEM((count, cols, width), F32)],
        ),
        out_shape=jax.ShapeDtypeStruct((count, cols, width), BF16),
        compiler_params=pltpu.CompilerParams(vmem_limit_bytes=VMEM),
        cost_estimate=pl.CostEstimate(
            flops=2 * count * rows * cols * width,
            bytes_accessed=2 * rows * (count * width + cols),
            transcendentals=0,
        ),
        name="mate_products",
    )(half, blocks, mate)


def pick(refs, which, index, into_ref):
    for at, ref in enumerate(refs):

        @pl.when(which == at)
        def _(ref=ref):
            into_ref[...] = ref[index].astype(into_ref.dtype)


def start_kernel(count, kind_ref, row_ref, col_ref, *refs):
    own_ref = refs[0]
    sent = {1: refs[1 : 1 + count], 2: refs[1 + 2 * count : 1 + 3 * count]}
    got = {1: refs[1 + count : 1 + 2 * count], 2: refs[1 + 3 * count : 1 + 4 * count]}
    inverse_ref, base_ref, rounded_ref, direct_ref, turned_ref = refs[1 + 4 * count :]
    slot = pl.program_id(0)
    kind, row, col = kind_ref[slot], row_ref[slot], col_ref[slot]

    @pl.when(kind == 0)
    def _():
        low, high = jnp.minimum(row, col), jnp.maximum(row, col)
        at = low * count - low * (low + 1) // 2 + high - low - 1
        value = own_ref[at].astype(F32)

        @pl.when(row < col)
        def _():
            direct_ref[...] = value
            turned_ref[...] = jnp.zeros_like(turned_ref)

        @pl.when(row > col)
        def _():
            direct_ref[...] = jnp.zeros_like(direct_ref)
            turned_ref[...] = value

    for which in (1, 2):

        @pl.when(kind == which)
        def _(which=which):
            pick(got[which], row, col, direct_ref)
            pick(sent[which], col, row, turned_ref)

    integral = direct_ref[...] + turned_ref[...].T
    base = -integral * inverse_ref[0]
    base_ref[0] = base
    rounded_ref[0] = base.astype(BF16)


def start_amplitudes(kind, row, col, own, chip_sent, chip_got, line_sent, line_got, inverse):
    slots, width, _ = inverse.shape
    count = len(chip_sent)
    tables = [own, *chip_sent, *chip_got, *line_sent, *line_got]
    whole = [pl.BlockSpec(t.shape, lambda s, *_: (0, 0, 0)) for t in tables]
    per_slot = pl.BlockSpec((1, width, width), lambda s, *_: (s, 0, 0))
    return pl.pallas_call(
        functools.partial(start_kernel, count),
        grid_spec=pltpu.PrefetchScalarGridSpec(
            num_scalar_prefetch=3,
            grid=(slots,),
            in_specs=[*whole, per_slot],
            out_specs=[per_slot, per_slot],
            scratch_shapes=[pltpu.VMEM((width, width), F32), pltpu.VMEM((width, width), F32)],
        ),
        out_shape=[
            jax.ShapeDtypeStruct((slots, width, width), F32),
            jax.ShapeDtypeStruct((slots, width, width), BF16),
        ],
        compiler_params=pltpu.CompilerParams(vmem_limit_bytes=VMEM),
        cost_estimate=pl.CostEstimate(flops=8 * slots * width * width, bytes_accessed=12 * 1024 * 1024, transcendentals=0),
        name="start_amplitudes",
    )(kind, row, col, *tables, inverse)


def sweep_kernel(kind_ref, source_ref, weight_ref, own_ref, chip_ref, line_ref, rows_ref, cols_ref, base_ref, inverse_ref, out_ref, picked_ref):
    slot = pl.program_id(0)
    total = None
    for n in range(rows_ref.shape[1]):
        pick((own_ref, chip_ref, line_ref), kind_ref[slot, n], source_ref[slot, n], picked_ref.at[n])
        selected = jnp.dot(rows_ref[0, n], picked_ref[n], preferred_element_type=F32).astype(BF16)
        term = weight_ref[slot, n] * jnp.dot(selected, cols_ref[0, n], preferred_element_type=F32)
        total = term if total is None else total + term
    out_ref[0] = (base_ref[0] + total * inverse_ref[0]).astype(out_ref.dtype)


def sweep_amplitudes(kind, source, weights, own, chip, line, row_match, col_match, base, inverse):
    slots, width, _ = own.shape
    neighbours = kind.shape[1]
    whole = pl.BlockSpec(own.shape, lambda s, *_: (0, 0, 0))
    match = pl.BlockSpec((1, neighbours, width, width), lambda s, *_: (s, 0, 0, 0))
    per_slot = pl.BlockSpec((1, width, width), lambda s, *_: (s, 0, 0))
    return pl.pallas_call(
        sweep_kernel,
        grid_spec=pltpu.PrefetchScalarGridSpec(
            num_scalar_prefetch=2,
            grid=(slots,),
            in_specs=[pl.BlockSpec(memory_space=pltpu.SMEM), whole, whole, whole, match, match, per_slot, per_slot],
            out_specs=per_slot,
            scratch_shapes=[pltpu.VMEM((neighbours, width, width), BF16)],
        ),
        out_shape=jax.ShapeDtypeStruct((slots, width, width), BF16),
        compiler_params=pltpu.CompilerParams(vmem_limit_bytes=VMEM),
        cost_estimate=pl.CostEstimate(
            flops=4 * slots * neighbours * width**3, bytes_accessed=16 * 1024 * 1024, transcendentals=0
        ),
        name="sweep_amplitudes",
    )(kind, source, weights, own, chip, line, row_match, col_match, base, inverse)


def on_device(three_index, pair_orbs, live_pairs, domains, coupled, fock_coupling_weight, occ_energy, virt_energy):
    count, naux, width = three_index.shape
    slots = coupled.shape[0]
    half_rows = naux // 2
    owner = lax.axis_index(LINE)
    parity = lax.axis_index("occ")
    chip_owner = owner + 1 - 2 * parity
    half = jnp.reshape(parity, (1,)).astype(jnp.int32)

    halves = three_index.reshape(count, 2, half_rows, width)
    sends = [lax.dynamic_index_in_dim(halves[j], 1 - parity, 0, keepdims=False) for j in range(count)]
    from_line = [line_mate(s) for s in sends]
    from_chip = [chip_mate(s) for s in sends]

    own = aux_sum(own_products(three_index))
    chip_sent = [aux_sum(mate_products(half, three_index, m)) for m in from_chip]
    chip_got = [chip_mate(v) for v in chip_sent]
    line_sent = [aux_sum(mate_products(half, three_index, m)) for m in from_line]
    line_got = [line_mate(v) for v in line_sent]

    local = jnp.arange(slots, dtype=jnp.int32)
    pairs = lax.dynamic_slice_in_dim(pair_orbs, owner * slots, slots, 0)
    live = (local < live_pairs[owner]).astype(F32)[:, None, None]
    rows, cols = pairs[:, 0], pairs[:, 1]

    def kind_of(other):
        return jnp.where(other == owner, 0, jnp.where(other == chip_owner, 1, 2)).astype(jnp.int32)

    energies = virt_energy[domains]
    gaps = (
        energies[rows][:, :, None]
        + energies[cols][:, None, :]
        - occ_energy[rows][:, None, None]
        - occ_energy[cols][:, None, None]
    )
    inverse = live / gaps
    source_rows = domains[pair_orbs[coupled, 0]]
    source_cols = domains[pair_orbs[coupled, 1]]
    row_match = (domains[rows][:, None, :, None] == source_rows[:, :, None, :]).astype(BF16)
    col_match = (source_cols[:, :, :, None] == domains[cols][:, None, None, :]).astype(BF16)

    base, rounded = start_amplitudes(
        kind_of(cols // count), rows % count, cols % count, own, chip_sent, chip_got, line_sent, line_got, inverse
    )
    kind, source = kind_of(coupled // slots), coupled % slots
    for sweep in range(ITERS):
        rounded = sweep_amplitudes(
            kind, source, fock_coupling_weight, rounded, chip_mate(rounded), line_mate(rounded),
            row_match, col_match, base, inverse,
        )
    return rounded


def solution(mesh):
    return jax.shard_map(
        on_device,
        mesh=mesh,
        in_specs=(
            P(("groups", "pair", "occ"), "aux", None),
            P("groups", None),
            P("groups"),
            P("groups", None),
            P(("groups", "pair", "occ"), None),
            P(("groups", "pair", "occ"), None),
            P("groups"),
            P("groups"),
        ),
        out_specs=P(("groups", "pair", "occ"), None, None),
        check_vma=False,
    )
```

```python
import functools

import jax
import jax.numpy as jnp
from jax import lax
from jax.experimental import pallas as pl
from jax.experimental.pallas import tpu as pltpu
from jax.sharding import PartitionSpec as P

ITERS = 2
LINE = ("pair", "occ")
MIB = 1024 * 1024
F32 = jnp.float32
BF16 = jnp.bfloat16
ROWS = (((0,), (0,)), ((), ()))


def chip_mate(value):
    return lax.ppermute(value, "occ", [(0, 1), (1, 0)])


def line_mate(value):
    pairs = []
    for chip in range(lax.axis_size("pair") - 1):
        left, right = 2 * chip + 1, 2 * chip + 2
        pairs += [(left, right), (right, left)]
    return lax.ppermute(value, LINE, pairs)


def aux_terms(value):
    count = lax.axis_size("aux")
    step = 1
    while True:
        other = lax.ppermute(value, "aux", [(i, i ^ step) for i in range(count)])
        step *= 2
        if step >= count:
            return value, other
        value = (value.astype(F32) + other.astype(F32)).astype(BF16)


def in_vmem(count):
    return [pl.BlockSpec(memory_space=pltpu.VMEM)] * count


def in_smem(count):
    return [pl.BlockSpec(memory_space=pltpu.SMEM)] * count


def params(mib):
    return pltpu.CompilerParams(vmem_limit_bytes=mib * MIB)


def cost(flops, moved):
    return pl.CostEstimate(flops=flops, bytes_accessed=moved, transcendentals=0)


def tile_rows(rows):
    for tile in (2560, 1280, 1024, 640, 512, 256, 128):
        if rows % tile == 0:
            return tile
    return rows


def own_kernel(block_ref, out_ref):
    step = pl.program_id(0)

    @pl.when(step == 0)
    def _():
        out_ref[...] = jnp.zeros_like(out_ref)

    count = block_ref.shape[0]
    at = 0
    for left in range(count):
        for right in range(left + 1, count):
            out_ref[at] += lax.dot_general(block_ref[left], block_ref[right], ROWS, preferred_element_type=F32)
            at += 1


def own_products(blocks):
    count, rows, width = blocks.shape
    tile = tile_rows(rows)
    combos = count * (count - 1) // 2
    return pl.pallas_call(
        own_kernel,
        grid=(rows // tile,),
        in_specs=[pl.BlockSpec((count, tile, width), lambda t: (0, t, 0))],
        out_specs=pl.BlockSpec((combos, width, width), lambda t: (0, 0, 0)),
        out_shape=jax.ShapeDtypeStruct((combos, width, width), F32),
        compiler_params=params(16),
        cost_estimate=cost(2 * combos * rows * width * width, 2 * count * rows * width),
        name="own_products",
    )(blocks)


def mate_kernel(block_ref, mate_ref, out_ref):
    for orb in range(block_ref.shape[0]):
        out_ref[orb] = lax.dot_general(
            mate_ref[...], block_ref[orb], ROWS, preferred_element_type=F32
        ).astype(out_ref.dtype)


def mate_products(blocks, mate, dtype):
    count, rows, width = blocks.shape
    cols = mate.shape[1]
    return pl.pallas_call(
        mate_kernel,
        in_specs=in_vmem(2),
        out_specs=in_vmem(1)[0],
        out_shape=jax.ShapeDtypeStruct((count, cols, width), dtype),
        compiler_params=params(16),
        cost_estimate=cost(2 * count * rows * cols * width, 2 * rows * (count * width + cols)),
        name="mate_products",
    )(blocks, mate)


def pick(pieces, refs, orbital, index, into_ref, add=False):
    for (owner, start, size), group in zip(pieces, refs, strict=True):

        @pl.when(orbital == owner)
        def _(start=start, size=size, group=group):
            value = group[0][index].astype(F32)
            for ref in group[1:]:
                value = value + ref[index].astype(F32)
            into_ref[start : start + size] = value


def local_kernel(pieces, count, kind_ref, row_ref, col_ref, own_ref, *refs):
    n = len(pieces)
    sent, got = [(r,) for r in refs[:n]], [(r,) for r in refs[n : 2 * n]]
    out_ref, direct_ref, turned_ref = refs[2 * n :]

    def body(slot, carry):
        kind, row, col = kind_ref[slot], row_ref[slot], col_ref[slot]

        @pl.when(kind == 0)
        def _():
            low, high = jnp.minimum(row, col), jnp.maximum(row, col)
            value = own_ref[low * count - low * (low + 1) // 2 + high - low - 1]

            @pl.when(row < col)
            def _():
                out_ref[slot] = value.astype(BF16)

            @pl.when(row > col)
            def _():
                out_ref[slot] = value.T.astype(BF16)

        @pl.when(kind == 1)
        def _():
            pick(pieces, got, row, col, direct_ref)
            pick(pieces, sent, col, row, turned_ref)
            out_ref[slot] = (direct_ref[...] + turned_ref[...].T).astype(BF16)

        @pl.when(kind == 2)
        def _():
            out_ref[slot] = jnp.zeros(out_ref.shape[1:], BF16)

        return carry

    lax.fori_loop(0, out_ref.shape[0], body, 0)


def local_integrals(pieces, kind, row, col, own, sent, got):
    slots, width, count = kind.shape[0], own.shape[-1], sent[0].shape[0]
    return pl.pallas_call(
        functools.partial(local_kernel, pieces, count),
        in_specs=in_smem(3) + in_vmem(1 + len(sent) + len(got)),
        out_specs=in_vmem(1)[0],
        out_shape=jax.ShapeDtypeStruct((slots, width, width), BF16),
        scratch_shapes=[pltpu.VMEM((width, width), F32), pltpu.VMEM((width, width), F32)],
        compiler_params=params(16),
        cost_estimate=cost(4 * slots * width * width, 8 * MIB),
        name="local_integrals",
    )(kind, row, col, own, *sent, *got)


def cross_kernel(pieces, kind_ref, row_ref, col_ref, inverse_ref, base_ref, *refs):
    n = len(pieces)
    sent, got = list(zip(refs[:n], refs[n : 2 * n], strict=True)), [(r,) for r in refs[2 * n : 3 * n]]
    out_ref, rounded_ref, direct_ref, turned_ref = refs[3 * n :]

    def body(slot, carry):
        kind, row, col = kind_ref[slot], row_ref[slot], col_ref[slot]

        @pl.when(kind == 2)
        def _():
            pick(pieces, got, row, col, direct_ref)
            pick(pieces, sent, col, row, turned_ref)
            value = -(direct_ref[...] + turned_ref[...].T) * inverse_ref[slot]
            out_ref[slot] = value
            rounded_ref[slot] = value.astype(BF16)

        @pl.when(kind != 2)
        def _():
            value = base_ref[slot]
            out_ref[slot] = value
            rounded_ref[slot] = value.astype(BF16)

        return carry

    lax.fori_loop(0, out_ref.shape[0], body, 0)


def cross_amplitudes(pieces, kind, row, col, inverse, base, sent, others, got):
    slots, width, _ = base.shape
    return pl.pallas_call(
        functools.partial(cross_kernel, pieces),
        in_specs=in_smem(3) + in_vmem(2 + len(sent) + len(others) + len(got)),
        out_specs=in_vmem(2),
        out_shape=[jax.ShapeDtypeStruct((slots, width, width), F32), jax.ShapeDtypeStruct((slots, width, width), BF16)],
        scratch_shapes=[pltpu.VMEM((width, width), F32), pltpu.VMEM((width, width), F32)],
        compiler_params=params(24),
        cost_estimate=cost(4 * slots * width * width, 8 * MIB),
        name="cross_amplitudes",
    )(kind, row, col, inverse, base, *sent, *others, *got)


def sweep_kernel(at_ref, weight_ref, own_ref, chip_ref, line_ref, rows_ref, cols_ref, base_ref, inverse_ref, out_ref, held_ref):
    slots, neighbours = rows_ref.shape[:2]
    held_ref[:slots] = own_ref[...]
    held_ref[slots : 2 * slots] = chip_ref[...]
    held_ref[2 * slots :] = line_ref[...]
    for slot in range(slots):
        total = None
        for n in range(neighbours):
            source = held_ref[at_ref[slot, n]]
            selected = jnp.dot(rows_ref[slot, n], source, preferred_element_type=F32).astype(BF16)
            term = weight_ref[slot, n] * jnp.dot(selected, cols_ref[slot, n], preferred_element_type=F32)
            total = term if total is None else total + term
        out_ref[slot] = (base_ref[slot] + total * inverse_ref[slot]).astype(out_ref.dtype)


def sweep_amplitudes(at, weights, own, chip, line, row_match, col_match, base, inverse):
    slots, width, _ = own.shape
    neighbours = at.shape[1]
    return pl.pallas_call(
        sweep_kernel,
        in_specs=in_smem(2) + in_vmem(7),
        out_specs=in_vmem(1)[0],
        out_shape=jax.ShapeDtypeStruct((slots, width, width), BF16),
        scratch_shapes=[pltpu.VMEM((3 * slots, width, width), BF16)],
        compiler_params=params(32),
        cost_estimate=cost(4 * slots * neighbours * width**3, 16 * MIB),
        name="sweep_amplitudes",
    )(at, weights, own, chip, line, row_match, col_match, base, inverse)


def on_device(three_index, pair_orbs, live_pairs, domains, coupled, fock_coupling_weight, occ_energy, virt_energy):
    count, naux, width = three_index.shape
    slots = coupled.shape[0]
    half_rows = naux // 2
    owner = lax.axis_index(LINE)
    parity = lax.axis_index("occ")
    chip_owner = owner + 1 - 2 * parity

    pieces = [(j, 0, width) for j in range(count - 1)]
    pieces += [(count - 1, 0, width // 2), (count - 1, width // 2, width // 2)]
    away = (1 - parity) * half_rows
    sends = [
        lax.dynamic_slice(three_index, (j, away, start), (1, half_rows, size)).reshape(half_rows, size)
        for j, start, size in pieces
    ]
    from_line = [line_mate(s) for s in sends]
    three_index, domains, pair_orbs, coupled, *sends = lax.optimization_barrier(
        (three_index, domains, pair_orbs, coupled, *sends)
    )
    own = own_products(three_index)
    own, *sends = lax.optimization_barrier((own, *sends))
    from_chip = [chip_mate(s) for s in sends]
    block = lax.dynamic_slice(three_index, (0, parity * half_rows, 0), (count, half_rows, width))

    local = jnp.arange(slots, dtype=jnp.int32)
    pairs = lax.dynamic_slice_in_dim(pair_orbs, owner * slots, slots, 0)
    live = (local < live_pairs[owner]).astype(F32)[:, None, None]
    rows, cols = pairs[:, 0], pairs[:, 1]
    row_dom, col_dom = domains[rows], domains[cols]

    def kind_of(other):
        return jnp.where(other == owner, 0, jnp.where(other == chip_owner, 1, 2)).astype(jnp.int32)

    def energy(dom):
        listed = jnp.arange(virt_energy.shape[0], dtype=jnp.int32)
        return jnp.sum(jnp.where(dom[..., None] == listed, virt_energy, 0.0), axis=-1)

    gaps = (
        energy(row_dom)[:, :, None]
        + energy(col_dom)[:, None, :]
        - occ_energy[rows][:, None, None]
        - occ_energy[cols][:, None, None]
    )
    inverse = live / gaps
    source_rows = domains[pair_orbs[coupled, 0]]
    source_cols = domains[pair_orbs[coupled, 1]]
    row_match = (row_dom[:, None, :, None] == source_rows[:, :, None, :]).astype(BF16)
    col_match = (source_cols[:, :, :, None] == col_dom[:, None, None, :]).astype(BF16)
    kind, row, col = kind_of(cols // count), rows % count, cols % count
    at = kind_of(coupled // slots) * slots + coupled % slots

    chip_sent = [mate_products(block, m, F32) for m in from_chip]
    chip_got = [chip_mate(v) for v in chip_sent]
    part, other = aux_terms(local_integrals(pieces, kind, row, col, own, chip_sent, chip_got))
    base = -(part.astype(F32) + other.astype(F32)) * inverse

    terms = [aux_terms(mate_products(block, m, BF16)) for m in from_line]
    got = [line_mate((a.astype(F32) + b.astype(F32)).astype(BF16)) for a, b in terms]
    base, rounded = cross_amplitudes(
        pieces, kind, row, col, inverse, base, [a for a, _ in terms], [b for _, b in terms], got
    )
    for sweep in range(ITERS):
        rounded = sweep_amplitudes(
            at, fock_coupling_weight, rounded, chip_mate(rounded), line_mate(rounded),
            row_match, col_match, base, inverse,
        )
    return rounded


def solution(mesh):
    return jax.shard_map(
        on_device,
        mesh=mesh,
        in_specs=(
            P(("groups", "pair", "occ"), "aux", None),
            P("groups", None),
            P("groups"),
            P("groups", None),
            P(("groups", "pair", "occ"), None),
            P(("groups", "pair", "occ"), None),
            P("groups"),
            P("groups"),
        ),
        out_specs=P(("groups", "pair", "occ"), None, None),
        check_vma=False,
    )
```

```python
import functools

import jax
import jax.numpy as jnp
from jax import lax
from jax.experimental import pallas as pl
from jax.experimental.pallas import tpu as pltpu
from jax.sharding import PartitionSpec as P

ITERS = 2
LINE = ("pair", "occ")
MIB = 1024 * 1024
F32 = jnp.float32
BF16 = jnp.bfloat16
ROWS = (((0,), (0,)), ((), ()))


def chip_mate(value):
    return lax.ppermute(value, "occ", [(0, 1), (1, 0)])


def line_mate(value):
    pairs = []
    for chip in range(lax.axis_size("pair") - 1):
        left, right = 2 * chip + 1, 2 * chip + 2
        pairs += [(left, right), (right, left)]
    return lax.ppermute(value, LINE, pairs)


def aux_terms(value):
    count = lax.axis_size("aux")
    step = 1
    while True:
        other = lax.ppermute(value, "aux", [(i, i ^ step) for i in range(count)])
        step *= 2
        if step >= count:
            return value, other
        value = (value.astype(F32) + other.astype(F32)).astype(BF16)


def in_vmem(count):
    return [pl.BlockSpec(memory_space=pltpu.VMEM)] * count


def in_smem(count):
    return [pl.BlockSpec(memory_space=pltpu.SMEM)] * count


def params(mib):
    return pltpu.CompilerParams(vmem_limit_bytes=mib * MIB)


def cost(flops, moved):
    return pl.CostEstimate(flops=flops // 1024, bytes_accessed=moved // 1024, transcendentals=0)


def after(value, *earlier):
    return lax.optimization_barrier((value, *earlier))[0]


CHUNKS = 2


def chunk(k, rows):
    return pl.ds(k * (rows // CHUNKS), rows // CHUNKS)


def half_chunk(half_ref, k, rows):
    size = rows // CHUNKS
    return pl.ds(pl.multiple_of(half_ref[0] * rows + k * size, size), size)


def tally(total_ref, out_ref, k, where, term):
    if k:
        term = term + total_ref[where]
    if k < CHUNKS - 1:
        total_ref[where] = term
    else:
        out_ref[where] = term.astype(out_ref.dtype)


def pairs_of(count):
    return [(i, j) for i in range(count) for j in range(i + 1, count)]


def send_kernel(half_ref, blocks_ref, *refs):
    count = blocks_ref.shape[0]
    sends, tail_ref, own_ref, block_ref, total_ref, arrived, written = refs[:count], *refs[count:]
    rows, cut = tail_ref.shape

    def read(k):
        block = blocks_ref.at[:, half_chunk(half_ref, k, rows)]
        return pltpu.make_async_copy(block, block_ref.at[:, chunk(k, rows)], arrived.at[k])

    def writes(k):
        part = chunk(k, rows)
        for j in range(count):
            yield pltpu.make_async_copy(block_ref.at[j, part], sends[j].at[part], written.at[k, j])
        tail = block_ref.at[count - 1, part, pl.ds(block_ref.shape[2] - cut, cut)]
        yield pltpu.make_async_copy(tail, tail_ref.at[part], written.at[k, count])

    for k in range(CHUNKS):
        read(k).start()
    for k in range(CHUNKS):
        read(k).wait()
        for copy in writes(k):
            copy.start()
        part = chunk(k, rows)
        for at, (i, j) in enumerate(pairs_of(count)):
            term = lax.dot_general(block_ref[i, part], block_ref[j, part], ROWS, preferred_element_type=F32)
            tally(total_ref, own_ref, k, at, term)
    for k in range(CHUNKS):
        for copy in writes(k):
            copy.wait()


def send_blocks(half, blocks, cut):
    count, rows, width = blocks.shape
    rows, combos = rows // 2, count * (count - 1) // 2
    anywhere = pl.BlockSpec(memory_space=pl.ANY)
    return pl.pallas_call(
        send_kernel,
        in_specs=in_smem(1) + [anywhere],
        out_specs=[anywhere] * (count + 1) + in_vmem(1),
        out_shape=[jax.ShapeDtypeStruct((rows, width), BF16)] * count
        + [jax.ShapeDtypeStruct((rows, cut), BF16), jax.ShapeDtypeStruct((combos, width, width), F32)],
        scratch_shapes=[
            pltpu.VMEM((count, rows, width), BF16),
            pltpu.VMEM((combos, width, width), F32),
            pltpu.SemaphoreType.DMA((CHUNKS,)),
            pltpu.SemaphoreType.DMA((CHUNKS, count + 1)),
        ],
        compiler_params=params(49),
        cost_estimate=cost(2 * combos * rows * width * width, 4 * count * rows * width),
        name="send_blocks",
    )(half, blocks)


def mate_kernel(n, with_own, half_ref, blocks_ref, *refs):
    mates, refs = refs[:n], refs[n:]
    if with_own:
        (away_ref, out_ref, own_ref), refs = refs[:3], refs[3:]
    else:
        out_ref, refs = refs[0], refs[1:]
    held, (block_ref, total_ref, arrived, *own_total) = refs[:n], refs[n:]
    count, rows, _ = block_ref.shape

    def copies(k):
        part = chunk(k, rows)
        block = blocks_ref.at[:, half_chunk(half_ref, k, rows)]
        yield pltpu.make_async_copy(block, block_ref.at[:, part], arrived.at[k, 0])
        for m in range(n):
            yield pltpu.make_async_copy(mates[m].at[part], held[m].at[part], arrived.at[k, m + 1])

    for k in range(CHUNKS):
        for copy in copies(k):
            copy.start()
    for k in range(CHUNKS):
        for copy in copies(k):
            copy.wait()
        part = chunk(k, rows)
        at = 0
        for mate_ref in held:
            cols = mate_ref.shape[1]
            for orb in range(count):
                term = lax.dot_general(mate_ref[part], block_ref[orb, part], ROWS, preferred_element_type=F32)
                tally(total_ref, out_ref, k, (orb, slice(at, at + cols)), term)
            at += cols
        if with_own:
            for at, (i, j) in enumerate(pairs_of(count)):
                term = lax.dot_general(block_ref[i, part], block_ref[j, part], ROWS, preferred_element_type=F32)
                if k == 0:
                    term = term + away_ref[at]
                tally(own_total[0], own_ref, k, at, term)


def mate_products(half, blocks, mates, away=None):
    count, rows, width = blocks.shape
    rows = rows // 2
    n, cols = len(mates), sum(m.shape[1] for m in mates)
    anywhere = pl.BlockSpec(memory_space=pl.ANY)
    out = [jax.ShapeDtypeStruct((count, cols, width), BF16)]
    own_total = []
    if away is not None:
        out.append(jax.ShapeDtypeStruct(away.shape, F32))
        own_total.append(pltpu.VMEM(away.shape, F32))
    results = pl.pallas_call(
        functools.partial(mate_kernel, n, away is not None),
        in_specs=in_smem(1) + [anywhere] * (1 + n) + in_vmem(len(out) - 1),
        out_specs=in_vmem(len(out)),
        out_shape=out,
        scratch_shapes=[
            *(pltpu.VMEM(m.shape, BF16) for m in mates),
            pltpu.VMEM((count, rows, width), BF16),
            pltpu.VMEM((count, cols, width), F32),
            pltpu.SemaphoreType.DMA((CHUNKS, n + 1)),
            *own_total,
        ],
        compiler_params=params(49),
        cost_estimate=cost(2 * count * rows * cols * width, 2 * rows * (count * width + cols)),
        name="mate_products",
    )(half, blocks, *mates, *([] if away is None else [away]))
    return results[0] if away is None else results


def local_kernel(kind_ref, row_ref, col_ref, own_ref, sent_ref, got_ref, out_ref):
    count, _, width = sent_ref.shape

    def rows_of(orbital):
        return pl.ds(pl.multiple_of(orbital * width, width), width)

    def body(slot, carry):
        kind, row, col = kind_ref[slot], row_ref[slot], col_ref[slot]

        @pl.when(kind == 0)
        def _():
            low, high = jnp.minimum(row, col), jnp.maximum(row, col)
            value = own_ref[low * count - low * (low + 1) // 2 + high - low - 1]

            @pl.when(row < col)
            def _():
                out_ref[slot] = value.astype(BF16)

            @pl.when(row > col)
            def _():
                out_ref[slot] = value.T.astype(BF16)

        @pl.when(kind == 1)
        def _():
            direct = got_ref[col, rows_of(row)].astype(F32)
            out_ref[slot] = (direct + sent_ref[row, rows_of(col)].astype(F32).T).astype(BF16)

        @pl.when(kind == 2)
        def _():
            out_ref[slot] = jnp.zeros(out_ref.shape[1:], BF16)

        return carry

    lax.fori_loop(0, out_ref.shape[0], body, 0)


def local_integrals(kind, row, col, own, sent, got):
    slots, width = kind.shape[0], own.shape[-1]
    return pl.pallas_call(
        local_kernel,
        in_specs=in_smem(3) + in_vmem(3),
        out_specs=in_vmem(1)[0],
        out_shape=jax.ShapeDtypeStruct((slots, width, width), BF16),
        compiler_params=params(8),
        cost_estimate=cost(4 * slots * width * width, 8 * MIB),
        name="local_integrals",
    )(kind, row, col, own, sent, got)


def pick(groups, refs, orbital, index, into_ref):
    for group, sources in zip(groups, refs, strict=True):
        at = 0
        for owner, start, size in group:

            @pl.when(orbital == owner)
            def _(at=at, start=start, size=size, sources=sources):
                value = sources[0][index, at : at + size].astype(F32)
                for ref in sources[1:]:
                    value = value + ref[index, at : at + size].astype(F32)
                into_ref[start : start + size] = value

            at += size


def cross_kernel(groups, kind_ref, row_ref, col_ref, inverse_ref, part_ref, other_ref, *refs):
    n = len(groups)
    sent, got = list(zip(refs[:n], refs[n : 2 * n], strict=True)), [(r,) for r in refs[2 * n : 3 * n]]
    base_ref, rounded_ref, direct_ref, turned_ref = refs[3 * n :]

    def body(slot, carry):
        kind, row, col = kind_ref[slot], row_ref[slot], col_ref[slot]

        def store(value):
            value = -value * inverse_ref[slot]
            base_ref[slot] = value
            rounded_ref[slot] = value.astype(BF16)

        @pl.when(kind == 2)
        def _():
            pick(groups, got, row, col, direct_ref)
            pick(groups, sent, col, row, turned_ref)
            store(direct_ref[...] + turned_ref[...].T)

        @pl.when(kind != 2)
        def _():
            store(part_ref[slot].astype(F32) + other_ref[slot].astype(F32))

        return carry

    lax.fori_loop(0, kind_ref.shape[0], body, 0)


def cross_amplitudes(groups, kind, row, col, inverse, local, sent, others, got):
    slots, width, _ = inverse.shape
    return pl.pallas_call(
        functools.partial(cross_kernel, groups),
        in_specs=in_smem(3) + in_vmem(3 + len(sent) + len(others) + len(got)),
        out_specs=in_vmem(2),
        out_shape=[jax.ShapeDtypeStruct((slots, width, width), F32), jax.ShapeDtypeStruct((slots, width, width), BF16)],
        scratch_shapes=[pltpu.VMEM((width, width), F32), pltpu.VMEM((width, width), F32)],
        compiler_params=params(8),
        cost_estimate=cost(4 * slots * width * width, 8 * MIB),
        name="cross_amplitudes",
    )(kind, row, col, inverse, *local, *sent, *others, *got)


def sweep_kernel(at_ref, weight_ref, own_ref, chip_ref, line_ref, rows_ref, cols_ref, base_ref, inverse_ref, out_ref, held_ref):
    slots, neighbours = rows_ref.shape[:2]
    held_ref[:slots] = own_ref[...]
    held_ref[slots : 2 * slots] = chip_ref[...]
    held_ref[2 * slots :] = line_ref[...]
    for slot in range(slots):
        total = None
        for n in range(neighbours):
            source = held_ref[at_ref[slot, n]]
            selected = jnp.dot(rows_ref[slot, n], source, preferred_element_type=F32).astype(BF16)
            term = weight_ref[slot, n] * jnp.dot(selected, cols_ref[slot, n], preferred_element_type=F32)
            total = term if total is None else total + term
        out_ref[slot] = (base_ref[slot] + total * inverse_ref[slot]).astype(out_ref.dtype)


def sweep_amplitudes(at, weights, own, chip, line, row_match, col_match, base, inverse):
    slots, width, _ = own.shape
    neighbours = at.shape[1]
    return pl.pallas_call(
        sweep_kernel,
        in_specs=in_smem(2) + in_vmem(7),
        out_specs=in_vmem(1)[0],
        out_shape=jax.ShapeDtypeStruct((slots, width, width), BF16),
        scratch_shapes=[pltpu.VMEM((3 * slots, width, width), BF16)],
        compiler_params=params(8),
        cost_estimate=cost(4 * slots * neighbours * width**3, 16 * MIB),
        name="sweep_amplitudes",
    )(at, weights, own, chip, line, row_match, col_match, base, inverse)


def on_device(three_index, pair_orbs, live_pairs, domains, coupled, fock_coupling_weight, occ_energy, virt_energy):
    count, naux, width = three_index.shape
    slots = coupled.shape[0]
    half_rows = naux // 2
    owner = lax.axis_index(LINE)
    parity = lax.axis_index("occ")
    chip_owner = owner + 1 - 2 * parity

    cut = width // 2
    head, tail = (count - 1, 0, cut), (count - 1, cut, width - cut)
    groups = [[head, (0, 0, width)], *[[(j, 0, width)] for j in range(1, count - 1)], [tail]]
    half = jnp.reshape(parity, (1,)).astype(jnp.int32)
    first = lax.dynamic_slice(three_index, (count - 1, (1 - parity) * half_rows, 0), (1, half_rows, cut))[0]
    *sends, last, own_away = send_blocks(1 - half, after(three_index, first), width - cut)
    from_line = [[line_mate(first), line_mate(sends[0])], *[[line_mate(s)] for s in sends[1:-1]], [line_mate(last)]]
    from_chip = [chip_mate(s) for s in sends]

    def total(terms, *earlier):
        a, b = lax.optimization_barrier((*terms, *earlier))[:2]
        return (a.astype(F32) + b.astype(F32)).astype(BF16)

    def cross_products(k, *earlier):
        mates = lax.optimization_barrier((*from_line[k], *earlier))[: len(from_line[k])]
        return mate_products(half, three_index, mates)

    domains, pair_orbs, coupled = lax.optimization_barrier((domains, pair_orbs, coupled, own_away, from_line[0][0]))[:3]

    local = jnp.arange(slots, dtype=jnp.int32)
    pairs = lax.dynamic_slice_in_dim(pair_orbs, owner * slots, slots, 0)
    live = (local < live_pairs[owner]).astype(F32)[:, None, None]
    rows, cols = pairs[:, 0], pairs[:, 1]
    row_dom, col_dom = domains[rows], domains[cols]

    def kind_of(other):
        return jnp.where(other == owner, 0, jnp.where(other == chip_owner, 1, 2)).astype(jnp.int32)

    def energy(dom):
        listed = jnp.arange(virt_energy.shape[0], dtype=jnp.int32)
        return jnp.sum(jnp.where(dom[..., None] == listed, virt_energy, 0.0), axis=-1)

    gaps = (
        energy(row_dom)[:, :, None]
        + energy(col_dom)[:, None, :]
        - occ_energy[rows][:, None, None]
        - occ_energy[cols][:, None, None]
    )
    inverse = live / gaps
    source_rows = domains[pair_orbs[coupled, 0]]
    source_cols = domains[pair_orbs[coupled, 1]]
    kind, row, col = kind_of(cols // count), rows % count, cols % count
    at = kind_of(coupled // slots) * slots + coupled % slots

    chip_sent, own = mate_products(half, after(three_index, inverse, source_rows, source_cols), from_chip, own_away)
    sent = [cross_products(0, chip_sent)]
    terms = [aux_terms(sent[0])]
    local = local_integrals(kind, row, col, own, chip_sent, after(chip_mate(chip_sent), sent[0]))
    local_terms = aux_terms(local)
    sums = []
    earlier = (local,)
    for k in range(1, len(groups)):
        sent.append(cross_products(k, *earlier))
        terms.append(aux_terms(sent[k]))
        sums.append(total(terms[k - 1], sent[k]))
        earlier = (sums[-1],)
    sums.append(total(terms[-1]))
    got = [line_mate(v) for v in sums]
    base, rounded = cross_amplitudes(
        groups, kind, row, col, inverse, local_terms, [a for a, _ in terms], [b for _, b in terms], got
    )
    row_dom, col_dom, source_rows, source_cols = lax.optimization_barrier(
        (row_dom, col_dom, source_rows, source_cols, rounded)
    )[:4]
    row_match = (row_dom[:, None, :, None] == source_rows[:, :, None, :]).astype(BF16)
    col_match = (source_cols[:, :, :, None] == col_dom[:, None, None, :]).astype(BF16)
    for sweep in range(ITERS):
        rounded = sweep_amplitudes(
            at, fock_coupling_weight, rounded, chip_mate(rounded), line_mate(rounded),
            row_match, col_match, base, inverse,
        )
    return rounded


def solution(mesh):
    return jax.shard_map(
        on_device,
        mesh=mesh,
        in_specs=(
            P(("groups", "pair", "occ"), "aux", None),
            P("groups", None),
            P("groups"),
            P("groups", None),
            P(("groups", "pair", "occ"), None),
            P(("groups", "pair", "occ"), None),
            P("groups"),
            P("groups"),
        ),
        out_specs=P(("groups", "pair", "occ"), None, None),
        check_vma=False,
    )
```

```python
import functools

import jax
import jax.numpy as jnp
from jax import lax
from jax.experimental import pallas as pl
from jax.experimental.pallas import tpu as pltpu
from jax.sharding import PartitionSpec as P

ITERS = 2
LINE = ("pair", "occ")
MIB = 1024 * 1024
F32 = jnp.float32
BF16 = jnp.bfloat16
ROWS = (((0,), (0,)), ((), ()))


def chip_mate(value):
    return lax.ppermute(value, "occ", [(0, 1), (1, 0)])


def line_mate(value):
    pairs = []
    for chip in range(lax.axis_size("pair") - 1):
        left, right = 2 * chip + 1, 2 * chip + 2
        pairs += [(left, right), (right, left)]
    return lax.ppermute(value, LINE, pairs)


def aux_terms(value):
    count = lax.axis_size("aux")
    step = 1
    while True:
        other = lax.ppermute(value, "aux", [(i, i ^ step) for i in range(count)])
        step *= 2
        if step >= count:
            return value, other
        value = (value.astype(F32) + other.astype(F32)).astype(BF16)


def in_vmem(count):
    return [pl.BlockSpec(memory_space=pltpu.VMEM)] * count


def in_smem(count):
    return [pl.BlockSpec(memory_space=pltpu.SMEM)] * count


def params(mib):
    return pltpu.CompilerParams(vmem_limit_bytes=mib * MIB)


def cost(flops, moved):
    return pl.CostEstimate(flops=flops // 1024, bytes_accessed=moved // 1024, transcendentals=0)


def after(value, *earlier):
    return lax.optimization_barrier((value, *earlier))[0]


CHUNKS = 2


def chunk(k, rows):
    return pl.ds(k * (rows // CHUNKS), rows // CHUNKS)


def half_chunk(half_ref, k, rows):
    size = rows // CHUNKS
    return pl.ds(pl.multiple_of(half_ref[0] * rows + k * size, size), size)


def tally(total_ref, out_ref, k, where, term):
    if k:
        term = term + total_ref[where]
    if k < CHUNKS - 1:
        total_ref[where] = term
    else:
        out_ref[where] = term.astype(out_ref.dtype)


def pairs_of(count):
    return [(i, j) for i in range(count) for j in range(i + 1, count)]


def send_kernel(half_ref, blocks_ref, *refs):
    count = blocks_ref.shape[0]
    sends, tail_ref, own_ref, block_ref, total_ref, arrived, written = refs[:count], *refs[count:]
    rows, cut = tail_ref.shape

    def read(k):
        block = blocks_ref.at[:, half_chunk(half_ref, k, rows)]
        return pltpu.make_async_copy(block, block_ref.at[:, chunk(k, rows)], arrived.at[k])

    def writes(k):
        part = chunk(k, rows)
        for j in range(count):
            yield pltpu.make_async_copy(block_ref.at[j, part], sends[j].at[part], written.at[k, j])
        tail = block_ref.at[count - 1, part, pl.ds(block_ref.shape[2] - cut, cut)]
        yield pltpu.make_async_copy(tail, tail_ref.at[part], written.at[k, count])

    for k in range(CHUNKS):
        read(k).start()
    for k in range(CHUNKS):
        read(k).wait()
        for copy in writes(k):
            copy.start()
        part = chunk(k, rows)
        for at, (i, j) in enumerate(pairs_of(count)):
            term = lax.dot_general(block_ref[i, part], block_ref[j, part], ROWS, preferred_element_type=F32)
            tally(total_ref, own_ref, k, at, term)
    for k in range(CHUNKS):
        for copy in writes(k):
            copy.wait()


def send_blocks(half, blocks, cut):
    count, rows, width = blocks.shape
    rows, combos = rows // 2, count * (count - 1) // 2
    anywhere = pl.BlockSpec(memory_space=pl.ANY)
    return pl.pallas_call(
        send_kernel,
        in_specs=in_smem(1) + [anywhere],
        out_specs=[anywhere] * (count + 1) + in_vmem(1),
        out_shape=[jax.ShapeDtypeStruct((rows, width), BF16)] * count
        + [jax.ShapeDtypeStruct((rows, cut), BF16), jax.ShapeDtypeStruct((combos, width, width), F32)],
        scratch_shapes=[
            pltpu.VMEM((count, rows, width), BF16),
            pltpu.VMEM((combos, width, width), F32),
            pltpu.SemaphoreType.DMA((CHUNKS,)),
            pltpu.SemaphoreType.DMA((CHUNKS, count + 1)),
        ],
        compiler_params=params(49),
        cost_estimate=cost(2 * combos * rows * width * width, 4 * count * rows * width),
        name="send_blocks",
    )(half, blocks)


def chip_kernel(n, half_ref, blocks_ref, *refs):
    mates, (away_ref, out_ref, own_ref, block_ref), refs = refs[:n], refs[n : n + 4], refs[n + 4 :]
    held, (total_ref, own_total_ref, arrived) = refs[:n], refs[n:]
    count, rows, width = block_ref.shape

    def copies(k):
        part = chunk(k, rows)
        block = blocks_ref.at[:, half_chunk(half_ref, k, rows)]
        yield pltpu.make_async_copy(block, block_ref.at[:, part], arrived.at[k, 0])
        for m in range(n):
            yield pltpu.make_async_copy(mates[m].at[part], held[m].at[part], arrived.at[k, m + 1])

    for k in range(CHUNKS):
        for copy in copies(k):
            copy.start()
    for k in range(CHUNKS):
        for copy in copies(k):
            copy.wait()
        part = chunk(k, rows)
        for m, mate_ref in enumerate(held):
            for orb in range(count):
                term = lax.dot_general(mate_ref[part], block_ref[orb, part], ROWS, preferred_element_type=F32)
                tally(total_ref, out_ref, k, (orb, slice(m * width, (m + 1) * width)), term)
        for at, (i, j) in enumerate(pairs_of(count)):
            term = lax.dot_general(block_ref[i, part], block_ref[j, part], ROWS, preferred_element_type=F32)
            if k == 0:
                term = term + away_ref[at]
            tally(own_total_ref, own_ref, k, at, term)


def chip_products(half, blocks, mates, away):
    count, rows, width = blocks.shape
    rows, n = rows // 2, len(mates)
    anywhere = pl.BlockSpec(memory_space=pl.ANY)
    return pl.pallas_call(
        functools.partial(chip_kernel, n),
        in_specs=in_smem(1) + [anywhere] * (1 + n) + in_vmem(1),
        out_specs=in_vmem(3),
        out_shape=[
            jax.ShapeDtypeStruct((count, n * width, width), BF16),
            jax.ShapeDtypeStruct(away.shape, F32),
            jax.ShapeDtypeStruct((count, rows, width), BF16),
        ],
        scratch_shapes=[
            *(pltpu.VMEM(m.shape, BF16) for m in mates),
            pltpu.VMEM((count, n * width, width), F32),
            pltpu.VMEM(away.shape, F32),
            pltpu.SemaphoreType.DMA((CHUNKS, n + 1)),
        ],
        compiler_params=params(40),
        cost_estimate=cost(2 * count * rows * n * width * width, 4 * rows * count * width),
        name="chip_products",
    )(half, blocks, *mates, away)


def line_kernel(n, block_ref, *refs):
    mates, out_ref, held, (total_ref, arrived) = refs[:n], refs[n], refs[n + 1 : 2 * n + 1], refs[2 * n + 1 :]
    count, rows, _ = block_ref.shape

    def copies(k):
        for m in range(n):
            part = chunk(k, rows)
            yield pltpu.make_async_copy(mates[m].at[part], held[m].at[part], arrived.at[k, m])

    for k in range(CHUNKS):
        for copy in copies(k):
            copy.start()
    for k in range(CHUNKS):
        for copy in copies(k):
            copy.wait()
        part = chunk(k, rows)
        at = 0
        for mate_ref in held:
            cols = mate_ref.shape[1]
            for orb in range(count):
                term = lax.dot_general(mate_ref[part], block_ref[orb, part], ROWS, preferred_element_type=F32)
                tally(total_ref, out_ref, k, (orb, slice(at, at + cols)), term)
            at += cols


def line_products(block, mates):
    count, rows, width = block.shape
    n, cols = len(mates), sum(m.shape[1] for m in mates)
    return pl.pallas_call(
        functools.partial(line_kernel, n),
        in_specs=in_vmem(1) + [pl.BlockSpec(memory_space=pl.ANY)] * n,
        out_specs=in_vmem(1)[0],
        out_shape=jax.ShapeDtypeStruct((count, cols, width), BF16),
        scratch_shapes=[
            *(pltpu.VMEM(m.shape, BF16) for m in mates),
            pltpu.VMEM((count, cols, width), F32),
            pltpu.SemaphoreType.DMA((CHUNKS, n)),
        ],
        compiler_params=params(10),
        cost_estimate=cost(2 * count * rows * cols * width, 2 * rows * (count * width + cols)),
        name="line_products",
    )(block, *mates)


def local_kernel(at_ref, own_ref, sent_ref, got_ref, out_ref):
    count, _, width = sent_ref.shape
    slots = out_ref.shape[0]

    def rows_of(orbital):
        return pl.ds(pl.multiple_of(orbital * width, width), width)

    def body(slot, carry):
        kind, row, col = at_ref[slot], at_ref[slots + slot], at_ref[2 * slots + slot]

        @pl.when(kind == 0)
        def _():
            low, high = jnp.minimum(row, col), jnp.maximum(row, col)
            value = own_ref[low * count - low * (low + 1) // 2 + high - low - 1]

            @pl.when(row < col)
            def _():
                out_ref[slot] = value.astype(BF16)

            @pl.when(row > col)
            def _():
                out_ref[slot] = value.T.astype(BF16)

        @pl.when(kind == 1)
        def _():
            direct = got_ref[col, rows_of(row)].astype(F32)
            out_ref[slot] = (direct + sent_ref[row, rows_of(col)].astype(F32).T).astype(BF16)

        @pl.when(kind == 2)
        def _():
            out_ref[slot] = jnp.zeros(out_ref.shape[1:], BF16)

        return carry

    lax.fori_loop(0, out_ref.shape[0], body, 0)


def local_integrals(slot_at, slots, own, sent, got):
    width = own.shape[-1]
    return pl.pallas_call(
        local_kernel,
        in_specs=in_smem(1) + in_vmem(3),
        out_specs=in_vmem(1)[0],
        out_shape=jax.ShapeDtypeStruct((slots, width, width), BF16),
        compiler_params=params(8),
        cost_estimate=cost(4 * slots * width * width, 8 * MIB),
        name="local_integrals",
    )(slot_at, own, sent, got)


def pick(groups, refs, orbital, index, into_ref):
    for group, sources in zip(groups, refs, strict=True):
        at = 0
        for owner, start, size in group:

            @pl.when(orbital == owner)
            def _(at=at, start=start, size=size, sources=sources):
                value = sources[0][index, at : at + size].astype(F32)
                for ref in sources[1:]:
                    value = value + ref[index, at : at + size].astype(F32)
                into_ref[start : start + size] = value

            at += size


def cross_kernel(groups, at_ref, row_gap_ref, col_gap_ref, inverse_ref, part_ref, other_ref, *refs):
    n = len(groups)
    sent, got = list(zip(refs[:n], refs[n : 2 * n], strict=True)), [(r,) for r in refs[2 * n : 3 * n]]
    base_ref, rounded_ref, mate_ref, direct_ref, turned_ref = refs[3 * n :]
    slots = rounded_ref.shape[0]

    def body(slot, carry):
        kind, row, col = at_ref[slot], at_ref[slots + slot], at_ref[2 * slots + slot]

        def store(value):
            value = -value * inverse_ref[slot]
            base_ref[slot] = value
            rounded_ref[slot] = value.astype(BF16)

        @pl.when(kind == 2)
        def _():
            pick(groups, got, row, col, direct_ref)
            pick(groups, sent, col, row, turned_ref)
            store(direct_ref[...] + turned_ref[...].T)

        @pl.when(kind != 2)
        def _():
            store(part_ref[slot].astype(F32) + other_ref[slot].astype(F32))

        row, col = at_ref[4 * slots + slot], at_ref[5 * slots + slot]

        @pl.when(at_ref[3 * slots + slot] == 1)
        def _():
            pick(groups, sent, row, col, direct_ref)
            pick(groups, got, col, row, turned_ref)
            gap = row_gap_ref[row] + col_gap_ref[col]
            mate_ref[slot] = (-(direct_ref[...] + turned_ref[...].T) / gap).astype(BF16)

        return carry

    lax.fori_loop(0, slots, body, 0)


def cross_amplitudes(groups, at, row_gap, col_gap, inverse, local, sent, others, got):
    slots, width, _ = inverse.shape
    return pl.pallas_call(
        functools.partial(cross_kernel, groups),
        in_specs=in_smem(1) + in_vmem(5 + len(sent) + len(others) + len(got)),
        out_specs=in_vmem(3),
        out_shape=[jax.ShapeDtypeStruct((slots, width, width), F32)]
        + [jax.ShapeDtypeStruct((slots, width, width), BF16)] * 2,
        scratch_shapes=[
            pltpu.VMEM((width, width), F32),
            pltpu.VMEM((width, width), F32),
        ],
        compiler_params=params(8),
        cost_estimate=cost(4 * slots * width * width, 8 * MIB),
        name="cross_amplitudes",
    )(at, row_gap, col_gap, inverse, *local, *sent, *others, *got)


def sweep_kernel(patched, at_ref, weight_ref, *refs):
    if patched:
        patch_at_ref, patch_ref, *refs = refs
    own_ref, chip_ref, line_ref, rows_ref, cols_ref, inverse_ref, base_ref, out_ref, held_ref = refs
    slots, neighbours = rows_ref.shape[:2]

    held_ref[:slots] = own_ref[...]
    held_ref[slots : 2 * slots] = chip_ref[...]
    held_ref[2 * slots :] = line_ref[...]
    if patched:

        def patch(slot, carry):
            @pl.when(patch_at_ref[3 * slots + slot] == 1)
            def _():
                held_ref[2 * slots + slot] = patch_ref[slot]

            return carry

        lax.fori_loop(0, slots, patch, 0)
    for slot in range(slots):
        total = None
        for n in range(neighbours):
            source = held_ref[at_ref[slot * neighbours + n]]
            selected = jnp.dot(rows_ref[slot, n], source, preferred_element_type=F32).astype(BF16)
            term = weight_ref[slot * neighbours + n] * jnp.dot(selected, cols_ref[slot, n], preferred_element_type=F32)
            total = term if total is None else total + term
        out_ref[slot] = (base_ref[slot] + total * inverse_ref[slot]).astype(out_ref.dtype)


def sweep_amplitudes(at, weights, own, chip, line, row_match, col_match, base, inverse, patch=()):
    slots, width, _ = own.shape
    neighbours = row_match.shape[1]
    return pl.pallas_call(
        functools.partial(sweep_kernel, bool(patch)),
        in_specs=in_smem(2 + len(patch[:1])) + in_vmem(7 + len(patch[1:])),
        out_specs=in_vmem(1)[0],
        out_shape=jax.ShapeDtypeStruct((slots, width, width), BF16),
        scratch_shapes=[pltpu.VMEM((3 * slots, width, width), BF16)],
        compiler_params=params(8),
        cost_estimate=cost(4 * slots * neighbours * width**3, 16 * MIB),
        name="sweep_amplitudes",
    )(at, weights, *patch, own, chip, line, row_match, col_match, inverse, base)


def on_device(three_index, pair_orbs, live_pairs, domains, coupled, fock_coupling_weight, occ_energy, virt_energy):
    count, naux, width = three_index.shape
    slots = coupled.shape[0]
    half_rows = naux // 2
    owner = lax.axis_index(LINE)
    parity = lax.axis_index("occ")
    chip_owner = owner + 1 - 2 * parity

    cut = width // 2
    head, tail = (count - 1, 0, cut), (count - 1, cut, width - cut)
    groups = [[head, (0, 0, width)], *[[(j, 0, width)] for j in range(1, count - 1)], [tail]]
    half = jnp.reshape(parity, (1,)).astype(jnp.int32)
    first = lax.dynamic_slice(three_index, (count - 1, (1 - parity) * half_rows, 0), (1, half_rows, cut))[0]
    *sends, last, own_away = send_blocks(1 - half, after(three_index, first), width - cut)
    from_line = [[line_mate(first), line_mate(sends[0])], *[[line_mate(s)] for s in sends[1:-1]], [line_mate(last)]]
    from_chip = [chip_mate(s) for s in sends]

    def total(terms, *earlier):
        a, b = lax.optimization_barrier((*terms, *earlier))[:2]
        return (a.astype(F32) + b.astype(F32)).astype(BF16)

    def cross_products(k, *earlier):
        mates = lax.optimization_barrier((*from_line[k], *earlier))[: len(from_line[k])]
        return line_products(block, mates)

    domains, pair_orbs, coupled = lax.optimization_barrier((domains, pair_orbs, coupled, own_away, from_line[0][0]))[:3]

    pairs = lax.dynamic_slice_in_dim(pair_orbs, owner * slots, slots, 0)
    line_owner = owner - 1 + 2 * parity
    mate_pairs = lax.dynamic_slice_in_dim(pair_orbs, line_owner * slots, slots, 0)
    rows, cols = pairs[:, 0], pairs[:, 1]
    row_dom, col_dom = domains[rows], domains[cols]

    def kind_of(other):
        return jnp.where(other == owner, 0, jnp.where(other == chip_owner, 1, 2)).astype(jnp.int32)

    seen = min(3 * count, domains.shape[0])
    window = jnp.clip((owner - 1) * count, 0, domains.shape[0] - seen)
    listed = jnp.arange(virt_energy.shape[0], dtype=jnp.int32)
    seen_dom = lax.dynamic_slice_in_dim(domains, window, seen, 0)
    seen_energy = jnp.sum(jnp.where(seen_dom[:, :, None] == listed, virt_energy, 0.0), axis=-1)
    seen_gap = seen_energy - lax.dynamic_slice_in_dim(occ_energy, window, seen, 0)[:, None]
    inverse = (jnp.arange(slots) < live_pairs[owner]).astype(F32)[:, None, None] / (
        seen_gap[rows - window][:, :, None] + seen_gap[cols - window][:, None, :]
    )
    own_gap = lax.dynamic_slice_in_dim(seen_gap, owner * count - window, count, 0)
    line_gap = lax.dynamic_slice_in_dim(seen_gap, line_owner * count - window, count, 0)
    row_gap = jnp.broadcast_to(line_gap[:, :, None], (count, width, width))
    source_rows = domains[pair_orbs[coupled, 0]]
    source_cols = domains[pair_orbs[coupled, 1]]
    kind, row, col = kind_of(cols // count), rows % count, cols % count
    inward = (
        (mate_pairs[:, 1] // count == owner)
        & (mate_pairs[:, 0] // count == line_owner)
        & (jnp.arange(slots) < live_pairs[line_owner])
    )
    slot_at = jnp.concatenate(
        [kind, row, col, inward.astype(jnp.int32), mate_pairs[:, 0] % count, mate_pairs[:, 1] % count]
    )
    at = (kind_of(coupled // slots) * slots + coupled % slots).reshape(-1)
    weights = fock_coupling_weight.reshape(-1)

    three_index, slot_at, at, weights, row_gap, own_gap, inverse, row_dom, col_dom, source_rows, source_cols = (
        lax.optimization_barrier(
            (three_index, slot_at, at, weights, row_gap, own_gap[:, None, :], inverse, row_dom, col_dom, source_rows, source_cols)
        )
    )
    chip_sent, own, block = chip_products(half, three_index, from_chip, own_away)
    local = local_integrals(slot_at, slots, own, chip_sent, chip_mate(chip_sent))
    local_terms = aux_terms(local)
    sent, terms, sums, got = [], [], [], []
    earlier = (local,)
    for k in range(len(groups)):
        sent.append(cross_products(k, *earlier))
        terms.append(aux_terms(sent[k]))
        if k == 1:
            part, other = lax.optimization_barrier((*local_terms, sent[1]))[:2]
            mate_start = (-(part.astype(F32) + other.astype(F32)) * inverse).astype(BF16)
        if k:
            sums.append(total(terms[k - 1], sent[k]))
            got.append(line_mate(sums[-1]))
        earlier = (sent[k], *([mate_start] if k == 1 else []), *(sums[-1:] if k else local_terms))
    sums.append(total(terms[-1], got[0]))
    got.append(line_mate(sums[-1]))
    from_mate = line_mate(after(mate_start, sums[-1]))
    base, rounded, patch = cross_amplitudes(
        groups, slot_at, row_gap, own_gap, inverse, local_terms,
        [a for a, _ in terms], [b for _, b in terms], got,
    )
    row_dom, col_dom, source_rows, source_cols = lax.optimization_barrier(
        (row_dom, col_dom, source_rows, source_cols, rounded)
    )[:4]
    row_match = (row_dom[:, None, :, None] == source_rows[:, :, None, :]).astype(BF16)
    col_match = (source_cols[:, :, :, None] == col_dom[:, None, None, :]).astype(BF16)
    for sweep in range(ITERS):
        from_line, patches = (line_mate(rounded), ()) if sweep else (from_mate, (slot_at, patch))
        rounded = sweep_amplitudes(
            at, weights, rounded, chip_mate(rounded), from_line, row_match, col_match, base, inverse, patches
        )
    return rounded


def solution(mesh):
    return jax.shard_map(
        on_device,
        mesh=mesh,
        in_specs=(
            P(("groups", "pair", "occ"), "aux", None),
            P("groups", None),
            P("groups"),
            P("groups", None),
            P(("groups", "pair", "occ"), None),
            P(("groups", "pair", "occ"), None),
            P("groups"),
            P("groups"),
        ),
        out_specs=P(("groups", "pair", "occ"), None, None),
        check_vma=False,
    )
```

```python
import functools

import jax
import jax.numpy as jnp
from jax import lax
from jax.experimental import pallas as pl
from jax.experimental.pallas import tpu as pltpu
from jax.sharding import PartitionSpec as P

ITERS = 2
LINE = ("pair", "occ")
MIB = 1024 * 1024
F32 = jnp.float32
BF16 = jnp.bfloat16
ROWS = (((0,), (0,)), ((), ()))


def chip_mate(value):
    return lax.ppermute(value, "occ", [(0, 1), (1, 0)])


def line_mate(value):
    pairs = []
    for chip in range(lax.axis_size("pair") - 1):
        left, right = 2 * chip + 1, 2 * chip + 2
        pairs += [(left, right), (right, left)]
    return lax.ppermute(value, LINE, pairs)


def aux_terms(value):
    count = lax.axis_size("aux")
    step = 1
    while True:
        other = lax.ppermute(value, "aux", [(i, i ^ step) for i in range(count)])
        step *= 2
        if step >= count:
            return value, other
        value = (value.astype(F32) + other.astype(F32)).astype(BF16)


def in_vmem(count):
    return [pl.BlockSpec(memory_space=pltpu.VMEM)] * count


def in_smem(count):
    return [pl.BlockSpec(memory_space=pltpu.SMEM)] * count


def params(mib):
    return pltpu.CompilerParams(vmem_limit_bytes=mib * MIB)


def cost(flops, moved):
    return pl.CostEstimate(flops=flops // 1024, bytes_accessed=moved // 1024, transcendentals=0)


def after(value, *earlier):
    return lax.optimization_barrier((value, *earlier))[0]


CHUNKS = 2
FILL = 60 * 10**9


def chunk(k, rows):
    return pl.ds(k * (rows // CHUNKS), rows // CHUNKS)


def half_chunk(half_ref, k, rows):
    size = rows // CHUNKS
    return pl.ds(pl.multiple_of(half_ref[0] * rows + k * size, size), size)


def tally(total_ref, out_ref, k, where, term):
    if k:
        term = term + total_ref[where]
    if k < CHUNKS - 1:
        total_ref[where] = term
    else:
        out_ref[where] = term.astype(out_ref.dtype)


def pairs_of(count):
    return [(i, j) for i in range(count) for j in range(i + 1, count)]


def send_kernel(half_ref, blocks_ref, *refs):
    count = blocks_ref.shape[0]
    sends, tail_ref, own_ref, block_ref, total_ref, arrived, written = refs[:count], *refs[count:]
    rows, cut = tail_ref.shape

    def read(k):
        block = blocks_ref.at[:, half_chunk(half_ref, k, rows)]
        return pltpu.make_async_copy(block, block_ref.at[:, chunk(k, rows)], arrived.at[k])

    def writes(k):
        part = chunk(k, rows)
        for j in range(count):
            yield pltpu.make_async_copy(block_ref.at[j, part], sends[j].at[part], written.at[k, j])
        tail = block_ref.at[count - 1, part, pl.ds(block_ref.shape[2] - cut, cut)]
        yield pltpu.make_async_copy(tail, tail_ref.at[part], written.at[k, count])

    for k in range(CHUNKS):
        read(k).start()
    for k in range(CHUNKS):
        read(k).wait()
        for copy in writes(k):
            copy.start()
        part = chunk(k, rows)
        for at, (i, j) in enumerate(pairs_of(count)):
            term = lax.dot_general(block_ref[i, part], block_ref[j, part], ROWS, preferred_element_type=F32)
            tally(total_ref, own_ref, k, at, term)
    for k in range(CHUNKS):
        for copy in writes(k):
            copy.wait()


def send_blocks(half, blocks, cut):
    count, rows, width = blocks.shape
    rows, combos = rows // 2, count * (count - 1) // 2
    anywhere = pl.BlockSpec(memory_space=pl.ANY)
    return pl.pallas_call(
        send_kernel,
        in_specs=in_smem(1) + [anywhere],
        out_specs=[anywhere] * (count + 1) + in_vmem(1),
        out_shape=[jax.ShapeDtypeStruct((rows, width), BF16)] * count
        + [jax.ShapeDtypeStruct((rows, cut), BF16), jax.ShapeDtypeStruct((combos, width, width), F32)],
        scratch_shapes=[
            pltpu.VMEM((count, rows, width), BF16),
            pltpu.VMEM((combos, width, width), F32),
            pltpu.SemaphoreType.DMA((CHUNKS,)),
            pltpu.SemaphoreType.DMA((CHUNKS, count + 1)),
        ],
        compiler_params=params(49),
        cost_estimate=cost(2 * combos * rows * width * width, 4 * count * rows * width),
        name="send_blocks",
    )(half, blocks)


def chip_kernel(n, half_ref, blocks_ref, *refs):
    mates, (away_ref, out_ref, own_ref, block_ref), refs = refs[:n], refs[n : n + 4], refs[n + 4 :]
    held, (total_ref, own_total_ref, arrived) = refs[:n], refs[n:]
    count, rows, width = block_ref.shape

    def copies(k):
        part = chunk(k, rows)
        block = blocks_ref.at[:, half_chunk(half_ref, k, rows)]
        yield pltpu.make_async_copy(block, block_ref.at[:, part], arrived.at[k, 0])
        for m in range(n):
            yield pltpu.make_async_copy(mates[m].at[part], held[m].at[part], arrived.at[k, m + 1])

    for k in range(CHUNKS):
        for copy in copies(k):
            copy.start()
    for k in range(CHUNKS):
        for copy in copies(k):
            copy.wait()
        part = chunk(k, rows)
        for m, mate_ref in enumerate(held):
            for orb in range(count):
                term = lax.dot_general(mate_ref[part], block_ref[orb, part], ROWS, preferred_element_type=F32)
                tally(total_ref, out_ref, k, (orb, slice(m * width, (m + 1) * width)), term)
        for at, (i, j) in enumerate(pairs_of(count)):
            term = lax.dot_general(block_ref[i, part], block_ref[j, part], ROWS, preferred_element_type=F32)
            if k == 0:
                term = term + away_ref[at]
            tally(own_total_ref, own_ref, k, at, term)


def chip_products(half, blocks, mates, away):
    count, rows, width = blocks.shape
    rows, n = rows // 2, len(mates)
    anywhere = pl.BlockSpec(memory_space=pl.ANY)
    return pl.pallas_call(
        functools.partial(chip_kernel, n),
        in_specs=in_smem(1) + [anywhere] * (1 + n) + in_vmem(1),
        out_specs=in_vmem(3),
        out_shape=[
            jax.ShapeDtypeStruct((count, n * width, width), BF16),
            jax.ShapeDtypeStruct(away.shape, F32),
            jax.ShapeDtypeStruct((count, rows, width), BF16),
        ],
        scratch_shapes=[
            *(pltpu.VMEM(m.shape, BF16) for m in mates),
            pltpu.VMEM((count, n * width, width), F32),
            pltpu.VMEM(away.shape, F32),
            pltpu.SemaphoreType.DMA((CHUNKS, n + 1)),
        ],
        compiler_params=params(40),
        cost_estimate=cost(2 * count * rows * n * width * width, 4 * rows * count * width),
        name="chip_products",
    )(half, blocks, *mates, away)


def line_kernel(n, block_ref, *refs):
    mates, out_ref, held, (total_ref, arrived) = refs[:n], refs[n], refs[n + 1 : 2 * n + 1], refs[2 * n + 1 :]
    count, rows, _ = block_ref.shape

    def copies(k):
        for m in range(n):
            part = chunk(k, rows)
            yield pltpu.make_async_copy(mates[m].at[part], held[m].at[part], arrived.at[k, m])

    for k in range(CHUNKS):
        for copy in copies(k):
            copy.start()
    for k in range(CHUNKS):
        for copy in copies(k):
            copy.wait()
        part = chunk(k, rows)
        at = 0
        for mate_ref in held:
            cols = mate_ref.shape[1]
            for orb in range(count):
                term = lax.dot_general(mate_ref[part], block_ref[orb, part], ROWS, preferred_element_type=F32)
                tally(total_ref, out_ref, k, (orb, slice(at, at + cols)), term)
            at += cols


def line_products(block, mates):
    count, rows, width = block.shape
    n, cols = len(mates), sum(m.shape[1] for m in mates)
    return pl.pallas_call(
        functools.partial(line_kernel, n),
        in_specs=in_vmem(1) + [pl.BlockSpec(memory_space=pl.ANY)] * n,
        out_specs=in_vmem(1)[0],
        out_shape=jax.ShapeDtypeStruct((count, cols, width), BF16),
        scratch_shapes=[
            *(pltpu.VMEM(m.shape, BF16) for m in mates),
            pltpu.VMEM((count, cols, width), F32),
            pltpu.SemaphoreType.DMA((CHUNKS, n)),
        ],
        compiler_params=params(10),
        cost_estimate=cost(2 * count * rows * cols * width, 2 * rows * (count * width + cols)),
        name="line_products",
    )(block, *mates)


def local_kernel(at_ref, own_ref, sent_ref, got_ref, out_ref):
    count, _, width = sent_ref.shape
    slots = out_ref.shape[0]

    def rows_of(orbital):
        return pl.ds(pl.multiple_of(orbital * width, width), width)

    def body(slot, carry):
        kind, row, col = at_ref[slot], at_ref[slots + slot], at_ref[2 * slots + slot]

        @pl.when(kind == 0)
        def _():
            low, high = jnp.minimum(row, col), jnp.maximum(row, col)
            value = own_ref[low * count - low * (low + 1) // 2 + high - low - 1]

            @pl.when(row < col)
            def _():
                out_ref[slot] = value.astype(BF16)

            @pl.when(row > col)
            def _():
                out_ref[slot] = value.T.astype(BF16)

        @pl.when(kind == 1)
        def _():
            direct = got_ref[col, rows_of(row)].astype(F32)
            out_ref[slot] = (direct + sent_ref[row, rows_of(col)].astype(F32).T).astype(BF16)

        @pl.when(kind == 2)
        def _():
            out_ref[slot] = jnp.zeros(out_ref.shape[1:], BF16)

        return carry

    lax.fori_loop(0, out_ref.shape[0], body, 0)


def local_integrals(slot_at, slots, own, sent, got):
    width = own.shape[-1]
    return pl.pallas_call(
        local_kernel,
        in_specs=in_smem(1) + in_vmem(3),
        out_specs=in_vmem(1)[0],
        out_shape=jax.ShapeDtypeStruct((slots, width, width), BF16),
        compiler_params=params(8),
        cost_estimate=cost(4 * slots * width * width, 8 * MIB),
        name="local_integrals",
    )(slot_at, own, sent, got)


def pick(groups, refs, orbital, index, into_ref):
    for group, sources in zip(groups, refs, strict=True):
        at = 0
        for owner, start, size in group:

            @pl.when(orbital == owner)
            def _(at=at, start=start, size=size, sources=sources):
                value = sources[0][index, at : at + size].astype(F32)
                for ref in sources[1:]:
                    value = value + ref[index, at : at + size].astype(F32)
                into_ref[start : start + size] = value

            at += size


def cross_kernel(groups, at_ref, row_gap_ref, col_gap_ref, inverse_ref, part_ref, other_ref, *refs):
    n = len(groups)
    sent, got = list(zip(refs[:n], refs[n : 2 * n], strict=True)), [(r,) for r in refs[2 * n : 3 * n]]
    base_ref, rounded_ref, mate_ref, direct_ref, turned_ref = refs[3 * n :]
    slots = rounded_ref.shape[0]

    def body(slot, carry):
        kind, row, col = at_ref[slot], at_ref[slots + slot], at_ref[2 * slots + slot]

        def store(value):
            value = -value * inverse_ref[slot]
            base_ref[slot] = value
            rounded_ref[slot] = value.astype(BF16)

        @pl.when(kind == 2)
        def _():
            pick(groups, got, row, col, direct_ref)
            pick(groups, sent, col, row, turned_ref)
            store(direct_ref[...] + turned_ref[...].T)

        @pl.when(kind != 2)
        def _():
            store(part_ref[slot].astype(F32) + other_ref[slot].astype(F32))

        row, col = at_ref[4 * slots + slot], at_ref[5 * slots + slot]

        @pl.when(at_ref[3 * slots + slot] == 1)
        def _():
            pick(groups, sent, row, col, direct_ref)
            pick(groups, got, col, row, turned_ref)
            gap = row_gap_ref[row] + col_gap_ref[col]
            mate_ref[slot] = (-(direct_ref[...] + turned_ref[...].T) / gap).astype(BF16)

        return carry

    lax.fori_loop(0, slots, body, 0)


def cross_amplitudes(groups, at, row_gap, col_gap, inverse, local, sent, others, got):
    slots, width, _ = inverse.shape
    return pl.pallas_call(
        functools.partial(cross_kernel, groups),
        in_specs=in_smem(1) + in_vmem(5 + len(sent) + len(others) + len(got)),
        out_specs=in_vmem(3),
        out_shape=[jax.ShapeDtypeStruct((slots, width, width), F32)]
        + [jax.ShapeDtypeStruct((slots, width, width), BF16)] * 2,
        scratch_shapes=[
            pltpu.VMEM((width, width), F32),
            pltpu.VMEM((width, width), F32),
        ],
        compiler_params=params(8),
        cost_estimate=cost(4 * slots * width * width, 8 * MIB),
        name="cross_amplitudes",
    )(at, row_gap, col_gap, inverse, *local, *sent, *others, *got)


def energy_kernel(energy_ref, dom_ref, out_ref):
    dom = dom_ref[...]

    def body(k, total):
        return jnp.where(dom == k, energy_ref[k], total)

    out_ref[...] = lax.fori_loop(0, energy_ref.shape[0], body, jnp.zeros(dom.shape, F32), unroll=8)


def energies_of(energies, dom):
    return pl.pallas_call(
        energy_kernel,
        in_specs=in_smem(1) + in_vmem(1),
        out_specs=in_vmem(1)[0],
        out_shape=jax.ShapeDtypeStruct(dom.shape, F32),
        compiler_params=params(8),
        cost_estimate=pl.CostEstimate(flops=FILL, bytes_accessed=0, transcendentals=0),
        name="energies_of",
    )(energies, dom)


def sweep_kernel(patched, at_ref, weight_ref, *refs):
    if patched:
        patch_at_ref, patch_ref, *refs = refs
    own_ref, chip_ref, line_ref, rows_ref, cols_ref, inverse_ref, base_ref, out_ref, held_ref = refs
    slots, neighbours = rows_ref.shape[:2]

    held_ref[:slots] = own_ref[...]
    held_ref[slots : 2 * slots] = chip_ref[...]
    held_ref[2 * slots :] = line_ref[...]
    if patched:

        def patch(slot, carry):
            @pl.when(patch_at_ref[3 * slots + slot] == 1)
            def _():
                held_ref[2 * slots + slot] = patch_ref[slot]

            return carry

        lax.fori_loop(0, slots, patch, 0)
    for slot in range(slots):
        total = None
        for n in range(neighbours):
            source = held_ref[at_ref[slot * neighbours + n]]
            selected = jnp.dot(rows_ref[slot, n], source, preferred_element_type=F32).astype(BF16)
            term = weight_ref[slot * neighbours + n] * jnp.dot(selected, cols_ref[slot, n], preferred_element_type=F32)
            total = term if total is None else total + term
        out_ref[slot] = (base_ref[slot] + total * inverse_ref[slot]).astype(out_ref.dtype)


def sweep_amplitudes(at, weights, own, chip, line, row_match, col_match, base, inverse, patch=()):
    slots, width, _ = own.shape
    neighbours = row_match.shape[1]
    return pl.pallas_call(
        functools.partial(sweep_kernel, bool(patch)),
        in_specs=in_smem(2 + len(patch[:1])) + in_vmem(7 + len(patch[1:])),
        out_specs=in_vmem(1)[0],
        out_shape=jax.ShapeDtypeStruct((slots, width, width), BF16),
        scratch_shapes=[pltpu.VMEM((3 * slots, width, width), BF16)],
        compiler_params=params(8),
        cost_estimate=cost(4 * slots * neighbours * width**3, 16 * MIB),
        name="sweep_amplitudes",
    )(at, weights, *patch, own, chip, line, row_match, col_match, inverse, base)


def on_device(three_index, pair_orbs, live_pairs, domains, coupled, fock_coupling_weight, occ_energy, virt_energy):
    count, naux, width = three_index.shape
    slots = coupled.shape[0]
    half_rows = naux // 2
    owner = lax.axis_index(LINE)
    parity = lax.axis_index("occ")
    chip_owner = owner + 1 - 2 * parity

    cut = width // 2
    head, tail = (count - 1, 0, cut), (count - 1, cut, width - cut)
    groups = [[head, (0, 0, width)], *[[(j, 0, width)] for j in range(1, count - 1)], [tail]]
    half = jnp.reshape(parity, (1,)).astype(jnp.int32)
    first = lax.dynamic_slice(three_index, (count - 1, (1 - parity) * half_rows, 0), (1, half_rows, cut))[0]
    *sends, last, own_away = send_blocks(1 - half, after(three_index, first), width - cut)
    from_line = [[line_mate(first), line_mate(sends[0])]]
    from_chip = [chip_mate(s) for s in sends]

    def total(terms, *earlier):
        a, b = lax.optimization_barrier((*terms, *earlier))[:2]
        return (a.astype(F32) + b.astype(F32)).astype(BF16)

    def cross_products(k, *earlier):
        mates = lax.optimization_barrier((*from_line[k], *earlier))[: len(from_line[k])]
        return line_products(block, mates)

    domains, pair_orbs, coupled = lax.optimization_barrier((domains, pair_orbs, coupled, own_away, from_line[0][0]))[:3]

    def kind_of(other):
        return jnp.where(other == owner, 0, jnp.where(other == chip_owner, 1, 2)).astype(jnp.int32)

    line_owner = owner - 1 + 2 * parity
    pairs = lax.dynamic_slice_in_dim(after(pair_orbs, own_away), owner * slots, slots, 0)
    rows, cols = pairs[:, 0], pairs[:, 1]
    slot_at = jnp.concatenate([kind_of(cols // count), rows % count, cols % count])
    seen = min(3 * count, domains.shape[0])
    window = jnp.clip((owner - 1) * count, 0, domains.shape[0] - seen)
    seen_dom = lax.dynamic_slice_in_dim(after(domains, own_away), window, seen, 0)
    seen_energy = energies_of(virt_energy, after(seen_dom, from_line[0][0], slot_at))

    chip_sent, own, block = chip_products(half, after(three_index, seen_energy), from_chip, own_away)
    local = local_integrals(slot_at, slots, own, chip_sent, chip_mate(chip_sent))
    local_terms = aux_terms(local)
    from_line += [[line_mate(s)] for s in sends[1:-1]]
    domains, pair_orbs, coupled, rows, cols, weights, seen_energy = lax.optimization_barrier(
        (domains, pair_orbs, coupled, rows, cols, fock_coupling_weight, seen_energy, local, from_line[0][1])
    )[:7]
    row_dom, col_dom = domains[rows], domains[cols]
    source_rows = domains[pair_orbs[coupled, 0]]
    source_cols = domains[pair_orbs[coupled, 1]]
    at = (kind_of(coupled // slots) * slots + coupled % slots).reshape(-1)
    seen_gap = seen_energy - lax.dynamic_slice_in_dim(occ_energy, window, seen, 0)[:, None]
    inverse = (jnp.arange(slots) < live_pairs[owner]).astype(F32)[:, None, None] / (
        seen_gap[rows - window][:, :, None] + seen_gap[cols - window][:, None, :]
    )
    own_gap = lax.dynamic_slice_in_dim(seen_gap, owner * count - window, count, 0)[:, None, :]
    row_gap = lax.dynamic_slice_in_dim(seen_gap, line_owner * count - window, count, 0)
    row_gap = jnp.broadcast_to(row_gap[:, :, None], (count, width, width))
    mate_pairs = lax.dynamic_slice_in_dim(pair_orbs, line_owner * slots, slots, 0)
    inward = (
        (mate_pairs[:, 1] // count == owner)
        & (mate_pairs[:, 0] // count == line_owner)
        & (jnp.arange(slots) < live_pairs[line_owner])
    )
    slot_at = jnp.concatenate(
        [slot_at, inward.astype(jnp.int32), mate_pairs[:, 0] % count, mate_pairs[:, 1] % count]
    )
    weights = weights.reshape(-1)
    tables = (row_dom, col_dom, source_rows, source_cols, at, inverse, own_gap, row_gap, slot_at, weights)

    sent, terms, sums, got = [], [], [], []
    earlier = tables
    for k in range(len(groups)):
        sent.append(cross_products(k, *earlier))
        terms.append(aux_terms(sent[k]))
        if k == 0:
            from_line.append([line_mate(after(last, sent[0]))])
        if k == 1:
            part, other = lax.optimization_barrier((*local_terms, sent[1]))[:2]
            mate_start = (-(part.astype(F32) + other.astype(F32)) * inverse).astype(BF16)
        if k:
            sums.append(total(terms[k - 1], sent[k]))
            got.append(line_mate(sums[-1]))
        earlier = (sent[k], *([mate_start] if k == 1 else []), *(sums[-1:] if k else local_terms))
    sums.append(total(terms[-1], got[0]))
    got.append(line_mate(sums[-1]))
    from_mate = line_mate(after(mate_start, sums[-1]))
    base, rounded, patch = cross_amplitudes(
        groups, slot_at, row_gap, own_gap, inverse, local_terms,
        [a for a, _ in terms], [b for _, b in terms], got,
    )
    row_dom, col_dom, source_rows, source_cols = lax.optimization_barrier(
        (row_dom, col_dom, source_rows, source_cols, rounded)
    )[:4]
    row_match = (row_dom[:, None, :, None] == source_rows[:, :, None, :]).astype(BF16)
    col_match = (source_cols[:, :, :, None] == col_dom[:, None, None, :]).astype(BF16)
    for sweep in range(ITERS):
        from_line, patches = (line_mate(rounded), ()) if sweep else (from_mate, (slot_at, patch))
        rounded = sweep_amplitudes(
            at, weights, rounded, chip_mate(rounded), from_line, row_match, col_match, base, inverse, patches
        )
    return rounded


def solution(mesh):
    return jax.shard_map(
        on_device,
        mesh=mesh,
        in_specs=(
            P(("groups", "pair", "occ"), "aux", None),
            P("groups", None),
            P("groups"),
            P("groups", None),
            P(("groups", "pair", "occ"), None),
            P(("groups", "pair", "occ"), None),
            P("groups"),
            P("groups"),
        ),
        out_specs=P(("groups", "pair", "occ"), None, None),
        check_vma=False,
    )
```

```python
import functools

import jax
import jax.numpy as jnp
from jax import lax
from jax.experimental import pallas as pl
from jax.experimental.pallas import tpu as pltpu
from jax.sharding import PartitionSpec as P

ITERS = 2
LINE = ("pair", "occ")
MIB = 1024 * 1024
F32 = jnp.float32
BF16 = jnp.bfloat16
ROWS = (((0,), (0,)), ((), ()))


def chip_mate(value):
    return lax.ppermute(value, "occ", [(0, 1), (1, 0)])


def line_mate(value):
    pairs = []
    for chip in range(lax.axis_size("pair") - 1):
        left, right = 2 * chip + 1, 2 * chip + 2
        pairs += [(left, right), (right, left)]
    return lax.ppermute(value, LINE, pairs)


def aux_terms(value):
    count = lax.axis_size("aux")
    step = 1
    while True:
        other = lax.ppermute(value, "aux", [(i, i ^ step) for i in range(count)])
        step *= 2
        if step >= count:
            return value, other
        value = (value.astype(F32) + other.astype(F32)).astype(BF16)


def in_vmem(count):
    return [pl.BlockSpec(memory_space=pltpu.VMEM)] * count


def in_smem(count):
    return [pl.BlockSpec(memory_space=pltpu.SMEM)] * count


def params(mib):
    return pltpu.CompilerParams(vmem_limit_bytes=mib * MIB)


def cost(flops, moved):
    return pl.CostEstimate(flops=flops // 1024, bytes_accessed=moved // 1024, transcendentals=0)


def after(value, *earlier):
    return lax.optimization_barrier((value, *earlier))[0]


CHUNKS = 2
FILL = 60 * 10**9


def chunk(k, rows):
    return pl.ds(k * (rows // CHUNKS), rows // CHUNKS)


def half_chunk(half_ref, k, rows):
    size = rows // CHUNKS
    return pl.ds(pl.multiple_of(half_ref[0] * rows + k * size, size), size)


def tally(total_ref, out_ref, k, where, term):
    if k:
        term = term + total_ref[where]
    if k < CHUNKS - 1:
        total_ref[where] = term
    else:
        out_ref[where] = term.astype(out_ref.dtype)


def pairs_of(count):
    return [(i, j) for i in range(count) for j in range(i + 1, count)]


def send_kernel(half_ref, blocks_ref, *refs):
    count = blocks_ref.shape[0]
    sends, tail_ref, own_ref, block_ref, total_ref, arrived, written = refs[:count], *refs[count:]
    rows, cut = tail_ref.shape

    def read(k):
        block = blocks_ref.at[:, half_chunk(half_ref, k, rows)]
        return pltpu.make_async_copy(block, block_ref.at[:, chunk(k, rows)], arrived.at[k])

    def writes(k):
        part = chunk(k, rows)
        for j in range(count):
            yield pltpu.make_async_copy(block_ref.at[j, part], sends[j].at[part], written.at[k, j])
        tail = block_ref.at[count - 1, part, pl.ds(block_ref.shape[2] - cut, cut)]
        yield pltpu.make_async_copy(tail, tail_ref.at[part], written.at[k, count])

    for k in range(CHUNKS):
        read(k).start()
    for k in range(CHUNKS):
        read(k).wait()
        for copy in writes(k):
            copy.start()
        part = chunk(k, rows)
        for at, (i, j) in enumerate(pairs_of(count)):
            term = lax.dot_general(block_ref[i, part], block_ref[j, part], ROWS, preferred_element_type=F32)
            tally(total_ref, own_ref, k, at, term)
    for k in range(CHUNKS):
        for copy in writes(k):
            copy.wait()


def send_blocks(half, blocks, cut):
    count, rows, width = blocks.shape
    rows, combos = rows // 2, count * (count - 1) // 2
    anywhere = pl.BlockSpec(memory_space=pl.ANY)
    return pl.pallas_call(
        send_kernel,
        in_specs=in_smem(1) + [anywhere],
        out_specs=[anywhere] * (count + 1) + in_vmem(1),
        out_shape=[jax.ShapeDtypeStruct((rows, width), BF16)] * count
        + [jax.ShapeDtypeStruct((rows, cut), BF16), jax.ShapeDtypeStruct((combos, width, width), F32)],
        scratch_shapes=[
            pltpu.VMEM((count, rows, width), BF16),
            pltpu.VMEM((combos, width, width), F32),
            pltpu.SemaphoreType.DMA((CHUNKS,)),
            pltpu.SemaphoreType.DMA((CHUNKS, count + 1)),
        ],
        compiler_params=params(49),
        cost_estimate=cost(2 * combos * rows * width * width, 4 * count * rows * width),
        name="send_blocks",
    )(half, blocks)


def chip_kernel(n, half_ref, blocks_ref, *refs):
    mates, (away_ref, out_ref, own_ref, block_ref), refs = refs[:n], refs[n : n + 4], refs[n + 4 :]
    held, (total_ref, own_total_ref, arrived) = refs[:n], refs[n:]
    count, rows, width = block_ref.shape

    def copies(k):
        part = chunk(k, rows)
        block = blocks_ref.at[:, half_chunk(half_ref, k, rows)]
        yield pltpu.make_async_copy(block, block_ref.at[:, part], arrived.at[k, 0])
        for m in range(n):
            yield pltpu.make_async_copy(mates[m].at[part], held[m].at[part], arrived.at[k, m + 1])

    for k in range(CHUNKS):
        for copy in copies(k):
            copy.start()
    for k in range(CHUNKS):
        for copy in copies(k):
            copy.wait()
        part = chunk(k, rows)
        for m, mate_ref in enumerate(held):
            for orb in range(count):
                term = lax.dot_general(mate_ref[part], block_ref[orb, part], ROWS, preferred_element_type=F32)
                tally(total_ref, out_ref, k, (orb, slice(m * width, (m + 1) * width)), term)
        for at, (i, j) in enumerate(pairs_of(count)):
            term = lax.dot_general(block_ref[i, part], block_ref[j, part], ROWS, preferred_element_type=F32)
            if k == 0:
                term = term + away_ref[at]
            tally(own_total_ref, own_ref, k, at, term)


def chip_products(half, blocks, mates, away):
    count, rows, width = blocks.shape
    rows, n = rows // 2, len(mates)
    anywhere = pl.BlockSpec(memory_space=pl.ANY)
    return pl.pallas_call(
        functools.partial(chip_kernel, n),
        in_specs=in_smem(1) + [anywhere] * (1 + n) + in_vmem(1),
        out_specs=in_vmem(3),
        out_shape=[
            jax.ShapeDtypeStruct((count, n * width, width), BF16),
            jax.ShapeDtypeStruct(away.shape, F32),
            jax.ShapeDtypeStruct((count, rows, width), BF16),
        ],
        scratch_shapes=[
            *(pltpu.VMEM(m.shape, BF16) for m in mates),
            pltpu.VMEM((count, n * width, width), F32),
            pltpu.VMEM(away.shape, F32),
            pltpu.SemaphoreType.DMA((CHUNKS, n + 1)),
        ],
        compiler_params=params(40),
        cost_estimate=cost(2 * count * rows * n * width * width, 4 * rows * count * width),
        name="chip_products",
    )(half, blocks, *mates, away)


def line_kernel(n, block_ref, *refs):
    mates, out_ref, held, (total_ref, arrived) = refs[:n], refs[n], refs[n + 1 : 2 * n + 1], refs[2 * n + 1 :]
    count, rows, _ = block_ref.shape

    def copies(k):
        for m in range(n):
            part = chunk(k, rows)
            yield pltpu.make_async_copy(mates[m].at[part], held[m].at[part], arrived.at[k, m])

    for k in range(CHUNKS):
        for copy in copies(k):
            copy.start()
    for k in range(CHUNKS):
        for copy in copies(k):
            copy.wait()
        part = chunk(k, rows)
        at = 0
        for mate_ref in held:
            cols = mate_ref.shape[1]
            for orb in range(count):
                term = lax.dot_general(mate_ref[part], block_ref[orb, part], ROWS, preferred_element_type=F32)
                tally(total_ref, out_ref, k, (orb, slice(at, at + cols)), term)
            at += cols


def line_products(block, mates):
    count, rows, width = block.shape
    n, cols = len(mates), sum(m.shape[1] for m in mates)
    return pl.pallas_call(
        functools.partial(line_kernel, n),
        in_specs=in_vmem(1) + [pl.BlockSpec(memory_space=pl.ANY)] * n,
        out_specs=in_vmem(1)[0],
        out_shape=jax.ShapeDtypeStruct((count, cols, width), BF16),
        scratch_shapes=[
            *(pltpu.VMEM(m.shape, BF16) for m in mates),
            pltpu.VMEM((count, cols, width), F32),
            pltpu.SemaphoreType.DMA((CHUNKS, n)),
        ],
        compiler_params=params(10),
        cost_estimate=cost(2 * count * rows * cols * width, 2 * rows * (count * width + cols)),
        name="line_products",
    )(block, *mates)


def local_kernel(at_ref, own_ref, sent_ref, got_ref, out_ref):
    count, _, width = sent_ref.shape
    slots = out_ref.shape[0]

    def rows_of(orbital):
        return pl.ds(pl.multiple_of(orbital * width, width), width)

    def body(slot, carry):
        kind, row, col = at_ref[slot], at_ref[slots + slot], at_ref[2 * slots + slot]

        @pl.when(kind == 0)
        def _():
            low, high = jnp.minimum(row, col), jnp.maximum(row, col)
            value = own_ref[low * count - low * (low + 1) // 2 + high - low - 1]

            @pl.when(row < col)
            def _():
                out_ref[slot] = value.astype(BF16)

            @pl.when(row > col)
            def _():
                out_ref[slot] = value.T.astype(BF16)

        @pl.when(kind == 1)
        def _():
            direct = got_ref[col, rows_of(row)].astype(F32)
            out_ref[slot] = (direct + sent_ref[row, rows_of(col)].astype(F32).T).astype(BF16)

        @pl.when(kind == 2)
        def _():
            out_ref[slot] = jnp.zeros(out_ref.shape[1:], BF16)

        return carry

    lax.fori_loop(0, out_ref.shape[0], body, 0)


def local_integrals(slot_at, slots, own, sent, got):
    width = own.shape[-1]
    return pl.pallas_call(
        local_kernel,
        in_specs=in_smem(1) + in_vmem(3),
        out_specs=in_vmem(1)[0],
        out_shape=jax.ShapeDtypeStruct((slots, width, width), BF16),
        compiler_params=params(8),
        cost_estimate=cost(4 * slots * width * width, 8 * MIB),
        name="local_integrals",
    )(slot_at, own, sent, got)


def pick(groups, refs, orbital, index, into_ref):
    for group, sources in zip(groups, refs, strict=True):
        at = 0
        for owner, start, size in group:

            @pl.when(orbital == owner)
            def _(at=at, start=start, size=size, sources=sources):
                value = sources[0][index, at : at + size].astype(F32)
                for ref in sources[1:]:
                    value = value + ref[index, at : at + size].astype(F32)
                into_ref[start : start + size] = value

            at += size


def cross_kernel(groups, at_ref, row_gap_ref, col_gap_ref, inverse_ref, part_ref, other_ref, *refs):
    n = len(groups)
    sent, got = list(zip(refs[:n], refs[n : 2 * n], strict=True)), [(r,) for r in refs[2 * n : 3 * n]]
    base_ref, rounded_ref, mate_ref, direct_ref, turned_ref = refs[3 * n :]
    slots = rounded_ref.shape[0]

    def body(slot, carry):
        kind, row, col = at_ref[slot], at_ref[slots + slot], at_ref[2 * slots + slot]

        def store(value):
            value = -value * inverse_ref[slot]
            base_ref[slot] = value
            rounded_ref[slot] = value.astype(BF16)

        @pl.when(kind == 2)
        def _():
            pick(groups, got, row, col, direct_ref)
            pick(groups, sent, col, row, turned_ref)
            store(direct_ref[...] + turned_ref[...].T)

        @pl.when(kind != 2)
        def _():
            store(part_ref[slot].astype(F32) + other_ref[slot].astype(F32))

        row, col = at_ref[4 * slots + slot], at_ref[5 * slots + slot]

        @pl.when(at_ref[3 * slots + slot] == 1)
        def _():
            pick(groups, sent, row, col, direct_ref)
            pick(groups, got, col, row, turned_ref)
            gap = row_gap_ref[row] + col_gap_ref[col]
            mate_ref[slot] = (-(direct_ref[...] + turned_ref[...].T) / gap).astype(BF16)

        return carry

    lax.fori_loop(0, slots, body, 0)


def cross_amplitudes(groups, at, row_gap, col_gap, inverse, local, sent, others, got):
    slots, width, _ = inverse.shape
    return pl.pallas_call(
        functools.partial(cross_kernel, groups),
        in_specs=in_smem(1) + in_vmem(5 + len(sent) + len(others) + len(got)),
        out_specs=in_vmem(3),
        out_shape=[jax.ShapeDtypeStruct((slots, width, width), F32)]
        + [jax.ShapeDtypeStruct((slots, width, width), BF16)] * 2,
        scratch_shapes=[
            pltpu.VMEM((width, width), F32),
            pltpu.VMEM((width, width), F32),
        ],
        compiler_params=params(8),
        cost_estimate=cost(4 * slots * width * width, 8 * MIB),
        name="cross_amplitudes",
    )(at, row_gap, col_gap, inverse, *local, *sent, *others, *got)


def energy_kernel(energy_ref, dom_ref, out_ref):
    dom = dom_ref[...]

    def body(k, total):
        return jnp.where(dom == k, energy_ref[k], total)

    out_ref[...] = lax.fori_loop(0, energy_ref.shape[0], body, jnp.zeros(dom.shape, F32), unroll=8)


def energies_of(energies, dom):
    return pl.pallas_call(
        energy_kernel,
        in_specs=in_smem(1) + in_vmem(1),
        out_specs=in_vmem(1)[0],
        out_shape=jax.ShapeDtypeStruct(dom.shape, F32),
        compiler_params=params(8),
        cost_estimate=pl.CostEstimate(flops=FILL, bytes_accessed=0, transcendentals=0),
        name="energies_of",
    )(energies, dom)


def near_kernel(at_ref, weight_ref, *refs):
    *parts, rows_ref, cols_ref, inverse_ref, base_ref, out_ref, held_ref = refs
    slots, neighbours = rows_ref.shape[:2]
    at = 0
    for part in parts:
        held_ref[at : at + part.shape[0]] = part[...]
        at += part.shape[0]
    for slot in range(slots):
        total = None
        for n in range(neighbours):
            at = at_ref[slot * neighbours + n]
            near = at < 2 * slots
            source = held_ref[jnp.where(near, at, 0)]
            weight = jnp.where(near, weight_ref[slot * neighbours + n], 0.0)
            selected = jnp.dot(rows_ref[slot, n], source, preferred_element_type=F32).astype(BF16)
            term = weight * jnp.dot(selected, cols_ref[slot, n], preferred_element_type=F32)
            total = term if total is None else total + term
        out_ref[slot] = base_ref[slot] + total * inverse_ref[slot]


def near_sweep(at, weights, parts, row_match, col_match, base, inverse):
    slots, width, _ = base.shape
    neighbours = row_match.shape[1]
    return pl.pallas_call(
        near_kernel,
        in_specs=in_smem(2) + in_vmem(4 + len(parts)),
        out_specs=in_vmem(1)[0],
        out_shape=jax.ShapeDtypeStruct((slots, width, width), F32),
        scratch_shapes=[pltpu.VMEM((2 * slots, width, width), BF16)],
        compiler_params=params(8),
        cost_estimate=cost(4 * slots * neighbours * width**3, 16 * MIB),
        name="near_sweep",
    )(at, weights, *parts, row_match, col_match, inverse, base)


GROUP = 4


def far_kernel(patched, at_ref, weight_ref, *refs):
    if patched:
        patch_at_ref, patch_ref, *refs = refs
    line_ref, rows_ref, cols_ref, inverse_ref, start_ref, out_ref, total_ref, list_ref = refs
    slots, neighbours = rows_ref.shape[:2]
    total_ref[...] = start_ref[...]

    def enlist(k, found):
        list_ref[found] = k
        return found + jnp.where(at_ref[k] >= 2 * slots, 1, 0)

    found = lax.fori_loop(0, slots * neighbours, enlist, 0)

    def product(k):
        slot, n = k // neighbours, k % neighbours
        mate_slot = at_ref[k] - 2 * slots
        source = line_ref[mate_slot]
        if patched:
            source = jnp.where(patch_at_ref[3 * slots + mate_slot] == 1, patch_ref[mate_slot], source)
        selected = jnp.dot(rows_ref[slot, n], source, preferred_element_type=F32).astype(BF16)
        return jnp.dot(selected, cols_ref[slot, n], preferred_element_type=F32)

    def body(step, carry):
        first = step * GROUP
        listed = [list_ref[jnp.minimum(first + g, found - 1)] for g in range(GROUP)]
        products = [product(k) for k in listed]
        for g, k in enumerate(listed):
            slot = k // neighbours
            weight = jnp.where(first + g < found, weight_ref[k], 0.0)
            total_ref[slot] += weight * products[g] * inverse_ref[slot]
        return carry

    lax.fori_loop(0, (found + GROUP - 1) // GROUP, body, 0)
    out_ref[...] = total_ref[...].astype(out_ref.dtype)


def far_sweep(at, weights, line, row_match, col_match, inverse, start, patch):
    slots, width, _ = line.shape
    neighbours = row_match.shape[1]
    return pl.pallas_call(
        functools.partial(far_kernel, bool(patch)),
        in_specs=in_smem(2 + len(patch[:1])) + in_vmem(5 + len(patch[1:])),
        out_specs=in_vmem(1)[0],
        out_shape=jax.ShapeDtypeStruct((slots, width, width), BF16),
        scratch_shapes=[pltpu.VMEM((slots, width, width), F32), pltpu.SMEM((slots * neighbours + 1,), jnp.int32)],
        compiler_params=params(8),
        cost_estimate=cost(4 * slots * neighbours * width**3, 16 * MIB),
        name="far_sweep",
    )(at, weights, *patch, line, row_match, col_match, inverse, start)


def on_device(three_index, pair_orbs, live_pairs, domains, coupled, fock_coupling_weight, occ_energy, virt_energy):
    count, naux, width = three_index.shape
    slots = coupled.shape[0]
    half_rows = naux // 2
    owner = lax.axis_index(LINE)
    parity = lax.axis_index("occ")
    chip_owner = owner + 1 - 2 * parity

    cut = width // 2
    head, tail = (count - 1, 0, cut), (count - 1, cut, width - cut)
    groups = [[head, (0, 0, width)], *[[(j, 0, width)] for j in range(1, count - 1)], [tail]]
    half = jnp.reshape(parity, (1,)).astype(jnp.int32)
    first = lax.dynamic_slice(three_index, (count - 1, (1 - parity) * half_rows, 0), (1, half_rows, cut))[0]
    *sends, last, own_away = send_blocks(1 - half, after(three_index, first), width - cut)
    from_line = [[line_mate(first), line_mate(sends[0])]]
    from_chip = [chip_mate(s) for s in sends]

    def total(terms, *earlier):
        a, b = lax.optimization_barrier((*terms, *earlier))[:2]
        return (a.astype(F32) + b.astype(F32)).astype(BF16)

    def cross_products(k, *earlier):
        mates = lax.optimization_barrier((*from_line[k], *earlier))[: len(from_line[k])]
        return line_products(block, mates)

    domains, pair_orbs, coupled = lax.optimization_barrier((domains, pair_orbs, coupled, own_away, from_line[0][0]))[:3]

    def kind_of(other):
        return jnp.where(other == owner, 0, jnp.where(other == chip_owner, 1, 2)).astype(jnp.int32)

    line_owner = owner - 1 + 2 * parity
    pairs = lax.dynamic_slice_in_dim(after(pair_orbs, own_away), owner * slots, slots, 0)
    rows, cols = pairs[:, 0], pairs[:, 1]
    slot_at = jnp.concatenate([kind_of(cols // count), rows % count, cols % count])
    seen = min(3 * count, domains.shape[0])
    window = jnp.clip((owner - 1) * count, 0, domains.shape[0] - seen)
    seen_dom = lax.dynamic_slice_in_dim(after(domains, own_away), window, seen, 0)
    seen_energy = energies_of(virt_energy, after(seen_dom, from_line[0][0], slot_at))

    chip_sent, own, block = chip_products(half, after(three_index, seen_energy), from_chip, own_away)
    local = local_integrals(slot_at, slots, own, chip_sent, chip_mate(chip_sent))
    local_terms = aux_terms(local)
    from_line += [[line_mate(s)] for s in sends[1:-1]]
    domains, pair_orbs, coupled, rows, cols, weights, seen_energy = lax.optimization_barrier(
        (domains, pair_orbs, coupled, rows, cols, fock_coupling_weight, seen_energy, local, from_line[0][1])
    )[:7]
    row_dom, col_dom = domains[rows], domains[cols]
    source_rows = domains[pair_orbs[coupled, 0]]
    source_cols = domains[pair_orbs[coupled, 1]]
    at = (kind_of(coupled // slots) * slots + coupled % slots).reshape(-1)
    seen_gap = seen_energy - lax.dynamic_slice_in_dim(occ_energy, window, seen, 0)[:, None]
    inverse = (jnp.arange(slots) < live_pairs[owner]).astype(F32)[:, None, None] / (
        seen_gap[rows - window][:, :, None] + seen_gap[cols - window][:, None, :]
    )
    own_gap = lax.dynamic_slice_in_dim(seen_gap, owner * count - window, count, 0)[:, None, :]
    row_gap = lax.dynamic_slice_in_dim(seen_gap, line_owner * count - window, count, 0)
    row_gap = jnp.broadcast_to(row_gap[:, :, None], (count, width, width))
    mate_pairs = lax.dynamic_slice_in_dim(pair_orbs, line_owner * slots, slots, 0)
    inward = (
        (mate_pairs[:, 1] // count == owner)
        & (mate_pairs[:, 0] // count == line_owner)
        & (jnp.arange(slots) < live_pairs[line_owner])
    )
    slot_at = jnp.concatenate(
        [slot_at, inward.astype(jnp.int32), mate_pairs[:, 0] % count, mate_pairs[:, 1] % count]
    )
    weights = weights.reshape(-1)
    tables = (row_dom, col_dom, source_rows, source_cols, at, inverse, own_gap, row_gap, slot_at, weights)

    sent, terms, sums, got = [], [], [], []
    earlier = tables
    for k in range(len(groups)):
        sent.append(cross_products(k, *earlier))
        terms.append(aux_terms(sent[k]))
        if k == 0:
            from_line.append([line_mate(after(last, sent[0]))])
        if k == 1:
            part, other = lax.optimization_barrier((*local_terms, sent[1]))[:2]
            mate_start = (-(part.astype(F32) + other.astype(F32)) * inverse).astype(BF16)
        if k:
            sums.append(total(terms[k - 1], sent[k]))
            got.append(line_mate(sums[-1]))
        earlier = (sent[k], *([mate_start] if k == 1 else []), *(sums[-1:] if k else local_terms))
    sums.append(total(terms[-1], got[0]))
    got.append(line_mate(sums[-1]))
    from_mate = line_mate(after(mate_start, sums[-1]))
    base, rounded, patch = cross_amplitudes(
        groups, slot_at, row_gap, own_gap, inverse, local_terms,
        [a for a, _ in terms], [b for _, b in terms], got,
    )
    row_dom, col_dom, source_rows, source_cols = lax.optimization_barrier(
        (row_dom, col_dom, source_rows, source_cols, rounded)
    )[:4]
    row_match = (row_dom[:, None, :, None] == source_rows[:, :, None, :]).astype(BF16)
    col_match = (source_cols[:, :, :, None] == col_dom[:, None, None, :]).astype(BF16)
    for sweep in range(ITERS):
        from_mate, patches = (line_mate(rounded), ()) if sweep else (from_mate, (slot_at, patch))
        cuts = (0, slots // 2, slots)
        chip = [chip_mate(rounded[i:j]) for i, j in zip(cuts[:-1], cuts[1:])]
        near = near_sweep(at, weights, [rounded, *chip], row_match, col_match, base, inverse)
        rounded = far_sweep(at, weights, after(from_mate, near), row_match, col_match, inverse, near, patches)
    return rounded


def solution(mesh):
    return jax.shard_map(
        on_device,
        mesh=mesh,
        in_specs=(
            P(("groups", "pair", "occ"), "aux", None),
            P("groups", None),
            P("groups"),
            P("groups", None),
            P(("groups", "pair", "occ"), None),
            P(("groups", "pair", "occ"), None),
            P("groups"),
            P("groups"),
        ),
        out_specs=P(("groups", "pair", "occ"), None, None),
        check_vma=False,
    )
```

```python
import functools

import jax
import jax.numpy as jnp
from jax import lax
from jax.experimental import pallas as pl
from jax.experimental.pallas import tpu as pltpu
from jax.sharding import PartitionSpec as P

ITERS = 2
LINE = ("pair", "occ")
MIB = 1024 * 1024
F32 = jnp.float32
BF16 = jnp.bfloat16
ROWS = (((0,), (0,)), ((), ()))


def chip_mate(value):
    return lax.ppermute(value, "occ", [(0, 1), (1, 0)])


def line_mate(value):
    pairs = []
    for chip in range(lax.axis_size("pair") - 1):
        left, right = 2 * chip + 1, 2 * chip + 2
        pairs += [(left, right), (right, left)]
    return lax.ppermute(value, LINE, pairs)


def aux_terms(value):
    count = lax.axis_size("aux")
    step = 1
    while True:
        other = lax.ppermute(value, "aux", [(i, i ^ step) for i in range(count)])
        step *= 2
        if step >= count:
            return value, other
        value = (value.astype(F32) + other.astype(F32)).astype(BF16)


def in_vmem(count):
    return [pl.BlockSpec(memory_space=pltpu.VMEM)] * count


def in_smem(count):
    return [pl.BlockSpec(memory_space=pltpu.SMEM)] * count


def params(mib):
    return pltpu.CompilerParams(vmem_limit_bytes=mib * MIB)


def cost(flops, moved):
    return pl.CostEstimate(flops=flops // 1024, bytes_accessed=moved // 1024, transcendentals=0)


def after(value, *earlier):
    return lax.optimization_barrier((value, *earlier))[0]


CHUNKS = 2
FILL = 60 * 10**9


def chunk(k, rows):
    return pl.ds(k * (rows // CHUNKS), rows // CHUNKS)


def half_chunk(half_ref, k, rows):
    size = rows // CHUNKS
    return pl.ds(pl.multiple_of(half_ref[0] * rows + k * size, size), size)


def tally(total_ref, out_ref, k, where, term):
    if k:
        term = term + total_ref[where]
    if k < CHUNKS - 1:
        total_ref[where] = term
    else:
        out_ref[where] = term.astype(out_ref.dtype)


def pairs_of(count):
    return [(i, j) for i in range(count) for j in range(i + 1, count)]


def send_kernel(half_ref, blocks_ref, *refs):
    count = blocks_ref.shape[0]
    sends, tail_ref, own_ref, block_ref, total_ref, arrived, written = refs[:count], *refs[count:]
    rows, cut = tail_ref.shape

    def read(k):
        block = blocks_ref.at[:, half_chunk(half_ref, k, rows)]
        return pltpu.make_async_copy(block, block_ref.at[:, chunk(k, rows)], arrived.at[k])

    def writes(k):
        part = chunk(k, rows)
        for j in range(count):
            yield pltpu.make_async_copy(block_ref.at[j, part], sends[j].at[part], written.at[k, j])
        tail = block_ref.at[count - 1, part, pl.ds(block_ref.shape[2] - cut, cut)]
        yield pltpu.make_async_copy(tail, tail_ref.at[part], written.at[k, count])

    for k in range(CHUNKS):
        read(k).start()
    for k in range(CHUNKS):
        read(k).wait()
        for copy in writes(k):
            copy.start()
        part = chunk(k, rows)
        for at, (i, j) in enumerate(pairs_of(count)):
            term = lax.dot_general(block_ref[i, part], block_ref[j, part], ROWS, preferred_element_type=F32)
            tally(total_ref, own_ref, k, at, term)
    for k in range(CHUNKS):
        for copy in writes(k):
            copy.wait()


def send_blocks(half, blocks, cut):
    count, rows, width = blocks.shape
    rows, combos = rows // 2, count * (count - 1) // 2
    anywhere = pl.BlockSpec(memory_space=pl.ANY)
    return pl.pallas_call(
        send_kernel,
        in_specs=in_smem(1) + [anywhere],
        out_specs=[anywhere] * (count + 1) + in_vmem(1),
        out_shape=[jax.ShapeDtypeStruct((rows, width), BF16)] * count
        + [jax.ShapeDtypeStruct((rows, cut), BF16), jax.ShapeDtypeStruct((combos, width, width), F32)],
        scratch_shapes=[
            pltpu.VMEM((count, rows, width), BF16),
            pltpu.VMEM((combos, width, width), F32),
            pltpu.SemaphoreType.DMA((CHUNKS,)),
            pltpu.SemaphoreType.DMA((CHUNKS, count + 1)),
        ],
        compiler_params=params(49),
        cost_estimate=cost(2 * combos * rows * width * width, 4 * count * rows * width),
        name="send_blocks",
    )(half, blocks)


def chip_kernel(n, half_ref, blocks_ref, *refs):
    mates, (away_ref, out_ref, own_ref, block_ref), refs = refs[:n], refs[n : n + 4], refs[n + 4 :]
    held, (total_ref, own_total_ref, arrived) = refs[:n], refs[n:]
    count, rows, width = block_ref.shape

    def copies(k):
        part = chunk(k, rows)
        block = blocks_ref.at[:, half_chunk(half_ref, k, rows)]
        yield pltpu.make_async_copy(block, block_ref.at[:, part], arrived.at[k, 0])
        for m in range(n):
            yield pltpu.make_async_copy(mates[m].at[part], held[m].at[part], arrived.at[k, m + 1])

    for k in range(CHUNKS):
        for copy in copies(k):
            copy.start()
    for k in range(CHUNKS):
        for copy in copies(k):
            copy.wait()
        part = chunk(k, rows)
        for m, mate_ref in enumerate(held):
            for orb in range(count):
                term = lax.dot_general(mate_ref[part], block_ref[orb, part], ROWS, preferred_element_type=F32)
                tally(total_ref, out_ref, k, (orb, slice(m * width, (m + 1) * width)), term)
        for at, (i, j) in enumerate(pairs_of(count)):
            term = lax.dot_general(block_ref[i, part], block_ref[j, part], ROWS, preferred_element_type=F32)
            if k == 0:
                term = term + away_ref[at]
            tally(own_total_ref, own_ref, k, at, term)


def chip_products(half, blocks, mates, away):
    count, rows, width = blocks.shape
    rows, n = rows // 2, len(mates)
    anywhere = pl.BlockSpec(memory_space=pl.ANY)
    return pl.pallas_call(
        functools.partial(chip_kernel, n),
        in_specs=in_smem(1) + [anywhere] * (1 + n) + in_vmem(1),
        out_specs=in_vmem(3),
        out_shape=[
            jax.ShapeDtypeStruct((count, n * width, width), BF16),
            jax.ShapeDtypeStruct(away.shape, F32),
            jax.ShapeDtypeStruct((count, rows, width), BF16),
        ],
        scratch_shapes=[
            *(pltpu.VMEM(m.shape, BF16) for m in mates),
            pltpu.VMEM((count, n * width, width), F32),
            pltpu.VMEM(away.shape, F32),
            pltpu.SemaphoreType.DMA((CHUNKS, n + 1)),
        ],
        compiler_params=params(40),
        cost_estimate=cost(2 * count * rows * n * width * width, 4 * rows * count * width),
        name="chip_products",
    )(half, blocks, *mates, away)


def line_kernel(n, block_ref, *refs):
    mates, out_ref, held, (total_ref, arrived) = refs[:n], refs[n], refs[n + 1 : 2 * n + 1], refs[2 * n + 1 :]
    count, rows, _ = block_ref.shape

    def copies(k):
        for m in range(n):
            part = chunk(k, rows)
            yield pltpu.make_async_copy(mates[m].at[part], held[m].at[part], arrived.at[k, m])

    for k in range(CHUNKS):
        for copy in copies(k):
            copy.start()
    for k in range(CHUNKS):
        for copy in copies(k):
            copy.wait()
        part = chunk(k, rows)
        at = 0
        for mate_ref in held:
            cols = mate_ref.shape[1]
            for orb in range(count):
                term = lax.dot_general(mate_ref[part], block_ref[orb, part], ROWS, preferred_element_type=F32)
                tally(total_ref, out_ref, k, (orb, slice(at, at + cols)), term)
            at += cols


def line_products(block, mates):
    count, rows, width = block.shape
    n, cols = len(mates), sum(m.shape[1] for m in mates)
    return pl.pallas_call(
        functools.partial(line_kernel, n),
        in_specs=in_vmem(1) + [pl.BlockSpec(memory_space=pl.ANY)] * n,
        out_specs=in_vmem(1)[0],
        out_shape=jax.ShapeDtypeStruct((count, cols, width), BF16),
        scratch_shapes=[
            *(pltpu.VMEM(m.shape, BF16) for m in mates),
            pltpu.VMEM((count, cols, width), F32),
            pltpu.SemaphoreType.DMA((CHUNKS, n)),
        ],
        compiler_params=params(10),
        cost_estimate=cost(2 * count * rows * cols * width, 2 * rows * (count * width + cols)),
        name="line_products",
    )(block, *mates)


def local_kernel(at_ref, own_ref, sent_ref, got_ref, out_ref):
    count, _, width = sent_ref.shape
    slots = out_ref.shape[0]

    def rows_of(orbital):
        return pl.ds(pl.multiple_of(orbital * width, width), width)

    def body(slot, carry):
        kind, row, col = at_ref[slot], at_ref[slots + slot], at_ref[2 * slots + slot]

        @pl.when(kind == 0)
        def _():
            low, high = jnp.minimum(row, col), jnp.maximum(row, col)
            value = own_ref[low * count - low * (low + 1) // 2 + high - low - 1]

            @pl.when(row < col)
            def _():
                out_ref[slot] = value.astype(BF16)

            @pl.when(row > col)
            def _():
                out_ref[slot] = value.T.astype(BF16)

        @pl.when(kind == 1)
        def _():
            direct = got_ref[col, rows_of(row)].astype(F32)
            out_ref[slot] = (direct + sent_ref[row, rows_of(col)].astype(F32).T).astype(BF16)

        @pl.when(kind == 2)
        def _():
            out_ref[slot] = jnp.zeros(out_ref.shape[1:], BF16)

        return carry

    lax.fori_loop(0, out_ref.shape[0], body, 0)


def local_integrals(slot_at, slots, own, sent, got):
    width = own.shape[-1]
    return pl.pallas_call(
        local_kernel,
        in_specs=in_smem(1) + in_vmem(3),
        out_specs=in_vmem(1)[0],
        out_shape=jax.ShapeDtypeStruct((slots, width, width), BF16),
        compiler_params=params(8),
        cost_estimate=cost(4 * slots * width * width, 8 * MIB),
        name="local_integrals",
    )(slot_at, own, sent, got)


def pick(groups, refs, orbital, index, into_ref):
    for group, sources in zip(groups, refs, strict=True):
        at = 0
        for owner, start, size in group:

            @pl.when(orbital == owner)
            def _(at=at, start=start, size=size, sources=sources):
                value = sources[0][index, at : at + size].astype(F32)
                for ref in sources[1:]:
                    value = value + ref[index, at : at + size].astype(F32)
                into_ref[start : start + size] = value

            at += size


def cross_kernel(groups, at_ref, row_gap_ref, col_gap_ref, inverse_ref, part_ref, other_ref, *refs):
    n = len(groups)
    sent, got = list(zip(refs[:n], refs[n : 2 * n], strict=True)), [(r,) for r in refs[2 * n : 3 * n]]
    base_ref, rounded_ref, mate_ref, direct_ref, turned_ref = refs[3 * n :]
    slots = rounded_ref.shape[0]

    def body(slot, carry):
        kind, row, col = at_ref[slot], at_ref[slots + slot], at_ref[2 * slots + slot]

        def store(value):
            value = -value * inverse_ref[slot]
            base_ref[slot] = value
            rounded_ref[slot] = value.astype(BF16)

        @pl.when(kind == 2)
        def _():
            pick(groups, got, row, col, direct_ref)
            pick(groups, sent, col, row, turned_ref)
            store(direct_ref[...] + turned_ref[...].T)

        @pl.when(kind != 2)
        def _():
            store(part_ref[slot].astype(F32) + other_ref[slot].astype(F32))

        row, col = at_ref[4 * slots + slot], at_ref[5 * slots + slot]

        @pl.when(at_ref[3 * slots + slot] == 1)
        def _():
            pick(groups, sent, row, col, direct_ref)
            pick(groups, got, col, row, turned_ref)
            gap = row_gap_ref[row] + col_gap_ref[col]
            mate_ref[slot] = (-(direct_ref[...] + turned_ref[...].T) / gap).astype(BF16)

        return carry

    lax.fori_loop(0, slots, body, 0)


def cross_amplitudes(groups, at, row_gap, col_gap, inverse, local, sent, others, got):
    slots, width, _ = inverse.shape
    return pl.pallas_call(
        functools.partial(cross_kernel, groups),
        in_specs=in_smem(1) + in_vmem(5 + len(sent) + len(others) + len(got)),
        out_specs=in_vmem(3),
        out_shape=[jax.ShapeDtypeStruct((slots, width, width), F32)]
        + [jax.ShapeDtypeStruct((slots, width, width), BF16)] * 2,
        scratch_shapes=[
            pltpu.VMEM((width, width), F32),
            pltpu.VMEM((width, width), F32),
        ],
        compiler_params=params(8),
        cost_estimate=cost(4 * slots * width * width, 8 * MIB),
        name="cross_amplitudes",
    )(at, row_gap, col_gap, inverse, *local, *sent, *others, *got)


def energy_kernel(energy_ref, dom_ref, out_ref):
    dom = dom_ref[...]

    def body(k, total):
        return jnp.where(dom == k, energy_ref[k], total)

    out_ref[...] = lax.fori_loop(0, energy_ref.shape[0], body, jnp.zeros(dom.shape, F32), unroll=8)


def energies_of(energies, dom):
    return pl.pallas_call(
        energy_kernel,
        in_specs=in_smem(1) + in_vmem(1),
        out_specs=in_vmem(1)[0],
        out_shape=jax.ShapeDtypeStruct(dom.shape, F32),
        compiler_params=params(8),
        cost_estimate=pl.CostEstimate(flops=FILL, bytes_accessed=0, transcendentals=0),
        name="energies_of",
    )(energies, dom)


def near_kernel(at_ref, weight_ref, *refs):
    *parts, rows_ref, cols_ref, inverse_ref, base_ref, out_ref, held_ref = refs
    slots, neighbours = rows_ref.shape[:2]
    at = 0
    for part in parts:
        held_ref[at : at + part.shape[0]] = part[...]
        at += part.shape[0]
    for slot in range(slots):
        total = None
        for n in range(neighbours):
            at = at_ref[slot * neighbours + n]
            near = at < 2 * slots
            source = held_ref[jnp.where(near, at, 0)]
            weight = jnp.where(near, weight_ref[slot * neighbours + n], 0.0)
            selected = jnp.dot(rows_ref[slot, n], source, preferred_element_type=F32).astype(BF16)
            term = weight * jnp.dot(selected, cols_ref[slot, n], preferred_element_type=F32)
            total = term if total is None else total + term
        out_ref[slot] = base_ref[slot] + total * inverse_ref[slot]


def near_sweep(at, weights, parts, row_match, col_match, base, inverse):
    slots, width, _ = base.shape
    neighbours = row_match.shape[1]
    return pl.pallas_call(
        near_kernel,
        in_specs=in_smem(2) + in_vmem(4 + len(parts)),
        out_specs=in_vmem(1)[0],
        out_shape=jax.ShapeDtypeStruct((slots, width, width), F32),
        scratch_shapes=[pltpu.VMEM((2 * slots, width, width), BF16)],
        compiler_params=params(8),
        cost_estimate=cost(4 * slots * neighbours * width**3, 16 * MIB),
        name="near_sweep",
    )(at, weights, *parts, row_match, col_match, inverse, base)


GROUP = 4


def far_kernel(patched, at_ref, weight_ref, *refs):
    if patched:
        patch_at_ref, patch_ref, *refs = refs
    line_ref, rows_ref, cols_ref, inverse_ref, start_ref, out_ref, total_ref, list_ref = refs
    slots, neighbours = rows_ref.shape[:2]
    total_ref[...] = start_ref[...]

    def enlist(k, found):
        list_ref[found] = k
        return found + jnp.where(at_ref[k] >= 2 * slots, 1, 0)

    found = lax.fori_loop(0, slots * neighbours, enlist, 0, unroll=True)

    def product(k):
        slot, n = k // neighbours, k % neighbours
        mate_slot = at_ref[k] - 2 * slots
        source = line_ref[mate_slot]
        if patched:
            source = jnp.where(patch_at_ref[3 * slots + mate_slot] == 1, patch_ref[mate_slot], source)
        selected = jnp.dot(rows_ref[slot, n], source, preferred_element_type=F32).astype(BF16)
        return jnp.dot(selected, cols_ref[slot, n], preferred_element_type=F32)

    def body(step, carry):
        first = step * GROUP
        listed = [list_ref[jnp.minimum(first + g, found - 1)] for g in range(GROUP)]
        products = [product(k) for k in listed]
        for g, k in enumerate(listed):
            slot = k // neighbours
            weight = jnp.where(first + g < found, weight_ref[k], 0.0)
            total_ref[slot] += weight * products[g] * inverse_ref[slot]
        return carry

    lax.fori_loop(0, (found + GROUP - 1) // GROUP, body, 0)
    out_ref[...] = total_ref[...].astype(out_ref.dtype)


def far_sweep(at, weights, line, row_match, col_match, inverse, start, patch):
    slots, width, _ = line.shape
    neighbours = row_match.shape[1]
    return pl.pallas_call(
        functools.partial(far_kernel, bool(patch)),
        in_specs=in_smem(2 + len(patch[:1])) + in_vmem(5 + len(patch[1:])),
        out_specs=in_vmem(1)[0],
        out_shape=jax.ShapeDtypeStruct((slots, width, width), BF16),
        scratch_shapes=[pltpu.VMEM((slots, width, width), F32), pltpu.SMEM((slots * neighbours + 1,), jnp.int32)],
        compiler_params=params(8),
        cost_estimate=cost(4 * slots * neighbours * width**3, 16 * MIB),
        name="far_sweep",
    )(at, weights, *patch, line, row_match, col_match, inverse, start)


def on_device(three_index, pair_orbs, live_pairs, domains, coupled, fock_coupling_weight, occ_energy, virt_energy):
    count, naux, width = three_index.shape
    slots = coupled.shape[0]
    half_rows = naux // 2
    owner = lax.axis_index(LINE)
    parity = lax.axis_index("occ")
    chip_owner = owner + 1 - 2 * parity

    cut = width // 2
    head, tail = (count - 1, 0, cut), (count - 1, cut, width - cut)
    groups = [[head, (0, 0, width)], *[[(j, 0, width)] for j in range(1, count - 1)], [tail]]
    half = jnp.reshape(parity, (1,)).astype(jnp.int32)
    first = lax.dynamic_slice(three_index, (count - 1, (1 - parity) * half_rows, 0), (1, half_rows, cut))[0]
    *sends, last, own_away = send_blocks(1 - half, after(three_index, first), width - cut)
    from_line = [[line_mate(first), line_mate(sends[0])]]
    from_chip = [chip_mate(s) for s in sends]

    def total(terms, *earlier):
        a, b = lax.optimization_barrier((*terms, *earlier))[:2]
        return (a.astype(F32) + b.astype(F32)).astype(BF16)

    def cross_products(k, *earlier):
        mates = lax.optimization_barrier((*from_line[k], *earlier))[: len(from_line[k])]
        return line_products(block, mates)

    domains, pair_orbs, coupled = lax.optimization_barrier((domains, pair_orbs, coupled, own_away, from_line[0][0]))[:3]

    def kind_of(other):
        return jnp.where(other == owner, 0, jnp.where(other == chip_owner, 1, 2)).astype(jnp.int32)

    line_owner = owner - 1 + 2 * parity
    pairs = lax.dynamic_slice_in_dim(after(pair_orbs, own_away), owner * slots, slots, 0)
    rows, cols = pairs[:, 0], pairs[:, 1]
    slot_at = jnp.concatenate([kind_of(cols // count), rows % count, cols % count])
    seen = min(3 * count, domains.shape[0])
    window = jnp.clip((owner - 1) * count, 0, domains.shape[0] - seen)
    seen_dom = lax.dynamic_slice_in_dim(after(domains, own_away), window, seen, 0)
    seen_energy = energies_of(virt_energy, after(seen_dom, from_line[0][0], slot_at))

    chip_sent, own, block = chip_products(half, after(three_index, seen_energy), from_chip, own_away)
    local = local_integrals(slot_at, slots, own, chip_sent, chip_mate(chip_sent))
    local_terms = aux_terms(local)
    from_line += [[line_mate(s)] for s in sends[1:-1]]
    domains, pair_orbs, coupled, rows, cols, weights, seen_energy = lax.optimization_barrier(
        (domains, pair_orbs, coupled, rows, cols, fock_coupling_weight, seen_energy, local, from_line[0][1])
    )[:7]
    row_dom, col_dom = domains[rows], domains[cols]
    source_rows = domains[pair_orbs[coupled, 0]]
    source_cols = domains[pair_orbs[coupled, 1]]
    at = (kind_of(coupled // slots) * slots + coupled % slots).reshape(-1)
    seen_gap = seen_energy - lax.dynamic_slice_in_dim(occ_energy, window, seen, 0)[:, None]
    inverse = (jnp.arange(slots) < live_pairs[owner]).astype(F32)[:, None, None] / (
        seen_gap[rows - window][:, :, None] + seen_gap[cols - window][:, None, :]
    )
    own_gap = lax.dynamic_slice_in_dim(seen_gap, owner * count - window, count, 0)[:, None, :]
    row_gap = lax.dynamic_slice_in_dim(seen_gap, line_owner * count - window, count, 0)
    row_gap = jnp.broadcast_to(row_gap[:, :, None], (count, width, width))
    mate_pairs = lax.dynamic_slice_in_dim(pair_orbs, line_owner * slots, slots, 0)
    inward = (
        (mate_pairs[:, 1] // count == owner)
        & (mate_pairs[:, 0] // count == line_owner)
        & (jnp.arange(slots) < live_pairs[line_owner])
    )
    slot_at = jnp.concatenate(
        [slot_at, inward.astype(jnp.int32), mate_pairs[:, 0] % count, mate_pairs[:, 1] % count]
    )
    weights = weights.reshape(-1)
    tables = (row_dom, col_dom, source_rows, source_cols, at, inverse, own_gap, row_gap, slot_at, weights)

    sent, terms, sums, got = [], [], [], []
    earlier = tables
    for k in range(len(groups)):
        sent.append(cross_products(k, *earlier))
        terms.append(aux_terms(sent[k]))
        if k == 0:
            from_line.append([line_mate(after(last, sent[0]))])
        if k == 1:
            part, other = lax.optimization_barrier((*local_terms, sent[1]))[:2]
            mate_start = (-(part.astype(F32) + other.astype(F32)) * inverse).astype(BF16)
        if k:
            sums.append(total(terms[k - 1], sent[k]))
            got.append(line_mate(sums[-1]))
        earlier = (sent[k], *([mate_start] if k == 1 else []), *(sums[-1:] if k else local_terms))
    sums.append(total(terms[-1], got[0]))
    got.append(line_mate(sums[-1]))
    from_mate = line_mate(after(mate_start, sums[-1]))
    base, rounded, patch = cross_amplitudes(
        groups, slot_at, row_gap, own_gap, inverse, local_terms,
        [a for a, _ in terms], [b for _, b in terms], got,
    )
    row_dom, col_dom, source_rows, source_cols = lax.optimization_barrier(
        (row_dom, col_dom, source_rows, source_cols, rounded)
    )[:4]
    row_match = (row_dom[:, None, :, None] == source_rows[:, :, None, :]).astype(BF16)
    col_match = (source_cols[:, :, :, None] == col_dom[:, None, None, :]).astype(BF16)
    for sweep in range(ITERS):
        from_mate, patches = (line_mate(rounded), ()) if sweep else (from_mate, (slot_at, patch))
        cuts = (0, slots // 2, slots)
        chip = [chip_mate(rounded[i:j]) for i, j in zip(cuts[:-1], cuts[1:])]
        near = near_sweep(at, weights, [rounded, *chip], row_match, col_match, base, inverse)
        rounded = far_sweep(at, weights, after(from_mate, near), row_match, col_match, inverse, near, patches)
    return rounded


def solution(mesh):
    return jax.shard_map(
        on_device,
        mesh=mesh,
        in_specs=(
            P(("groups", "pair", "occ"), "aux", None),
            P("groups", None),
            P("groups"),
            P("groups", None),
            P(("groups", "pair", "occ"), None),
            P(("groups", "pair", "occ"), None),
            P("groups"),
            P("groups"),
        ),
        out_specs=P(("groups", "pair", "occ"), None, None),
        check_vma=False,
    )
```
